32 devices in a mesh: cfg: 8 (over y, x, core), tm: 4 (over z).
Axes of the slice: x: 2, y: 2, z: 4, core: 2. Of those that a mesh axis runs over, the one named last changes fastest.
Arguments:
- targets: float32 [2048, 512], P('cfg', 'tm'), may hold values from -6 to 6
- features: float32 [2048, 64], P('cfg'), may hold values from -6 to 6
- inv_scales: float32 [64], replicated, may hold values from 0.05 to 0.3
- noise: float32 [2048], P('cfg'), may hold values from 0.1 to 1
- time_kernel: float32 [512, 512], P('tm'), may hold values from -1 to 1, as said below
- block_mask: int32 [2048, 4], P('cfg', 'tm'), may hold values from 0 to 1, as said below
Outputs:
- solution_field: float32 [2048, 512], P('cfg', 'tm')
- residual: float32 [2048, 512], P('cfg', 'tm')
The draws below stay inside these ranges and needn't reach their ends.
Inputs may be any that keep to these rules, and one draw needn't show every extreme that they name: `block_mask`: each configuration observes one contiguous run of blocks that starts at a block of 0 to 1 and has at least one block; some runs start late and some reach the last block. `time_kernel`: symmetric positive definite, with unit diagonal.
All inputs are finite; a program needn't handle non-finite values.
Results may differ from the reference program's by a relative error of at most 0.00026.
Values sent between devices are 32-bit elements; how exact they have to be, the bound alone decides.
No kernel may reach another device: no remote copies, remote signals or barrier semaphores. Data moves between devices by JAX's collectives and lax.ppermute only.
A program may use at most 64 MiB of HBM per device.

```python
import math
import jax
import jax.numpy as jnp
from jax import lax

F = 64
BLOCK = 128
ITERS = 2
NC = 2048
NT = 512
NB = 4


def draw_time_kernel(key, part):
    place_key, mix_key = jax.random.split(jax.random.fold_in(key, 29))
    increments = jax.random.uniform(place_key, (NT,), jnp.float32, 0.5, 1.5)
    factor = jax.random.normal(mix_key, (NT, 2 * NT), jnp.float32)
    places = jnp.cumsum(increments)
    smooth = jnp.exp(-jnp.abs(places[:, None] - places[None, :]) / (NT / 8.0))
    rough = jnp.dot(factor, factor.T, precision=lax.Precision.HIGHEST, preferred_element_type=jnp.float32) / (2.0 * NT)
    rough = 0.5 * (rough + rough.T)
    total = 0.5 * smooth + 0.5 * rough
    inverse_root = 1.0 / jnp.sqrt(jnp.diagonal(total))
    kernel = total * inverse_root[:, None] * inverse_root[None, :]
    kernel = 0.5 * (kernel + kernel.T)
    steps = jnp.arange(NT, dtype=jnp.int32)
    on_diagonal = steps[:, None] == steps[None, :]
    return jnp.where(on_diagonal, 1.0, jnp.clip(kernel, -1.0, 1.0)).astype(jnp.float32)


def draw_block_mask(key, part):
    first_key, second_key = jax.random.split(jax.random.fold_in(key, 17))
    begin = jax.random.randint(first_key, (NC,), 0, NB // 4 + 1)
    finish = jax.random.randint(second_key, (NC,), begin + 1, NB + 1)
    finish = finish.at[0].set(NB)
    begin = begin.at[1].set(NB // 4)
    finish = finish.at[1].set(NB // 4 + 1)
    blocks = jnp.arange(NB, dtype=jnp.int32)[None, :]
    return ((blocks >= begin[:, None]) & (blocks < finish[:, None])).astype(jnp.int32)


def block_scale(rng, extent, cuts, low, top_value):
    loudness, own = 1.0, jax.random.fold_in(rng, 6)
    for position, parts in cuts:
        steps = jnp.exp(jax.random.uniform(jax.random.fold_in(own, position), (parts,), jnp.float32, low / len(cuts), top_value / len(cuts)))
        loudness = loudness * jnp.repeat(steps, extent[position] // parts).reshape([-1 if axis == position else 1 for axis in range(len(extent))])
    return loudness


def bell_draw(own_key, extent, spread, most, shards=(), kind=jnp.bfloat16):
    level = block_scale(own_key, extent, shards, -0.22, 0.18) if shards else 1.0
    array = jax.random.normal(own_key, extent, jnp.float32) * spread * level
    return jnp.minimum(jnp.maximum(array, -most), most).astype(kind)


def setup_inputs(seed: int = 0) -> dict:
    keys = jax.random.split(jax.random.key(seed), 7)
    targets = bell_draw(keys[0], (NC, NT), 1.0, 6.0, ((0, 8), (1, 4)), jnp.float32)
    features = bell_draw(keys[1], (NC, F), 1.0, 6.0, ((0, 8),), jnp.float32)
    inv_scales = jnp.clip(jnp.exp(jax.random.uniform(keys[2], (F,), jnp.float32, math.log(0.05), math.log(0.3))), 0.05, 0.3)
    noise = jnp.clip(jnp.exp(math.log(1.0) - 2.3025851 * jax.random.uniform(keys[3], (NC,), jnp.float32) ** block_scale(keys[3], (NC,), ((0, 8),), -0.2, 0.2)), 0.1, 1.0)
    time_kernel = draw_time_kernel(jax.random.fold_in(keys[6], 71), 0)
    block_mask = draw_block_mask(jax.random.fold_in(keys[6], 71), 0)
    return {"targets": targets, "features": features, "inv_scales": inv_scales, "noise": noise, "time_kernel": time_kernel, "block_mask": block_mask}


def matern(left, right):
    cross = jnp.dot(left, right.T, precision=lax.Precision.HIGHEST, preferred_element_type=jnp.float32)
    dist2 = lax.optimization_barrier(jnp.sum(left * left, axis=1))[:, None] + lax.optimization_barrier(jnp.sum(right * right, axis=1))[None, :] - 2.0 * cross
    scaled_dist = jnp.sqrt(3.0) * jnp.sqrt(jnp.maximum(dist2, 0.0))
    return (1.0 + scaled_dist) * jnp.exp(-scaled_dist)

def reference(targets, features, inv_scales, noise, time_kernel, block_mask):
    count = targets.shape[0]
    mask = jnp.repeat(block_mask.astype(jnp.float32), BLOCK, axis=1)
    scaled = features * inv_scales[None, :]
    rowblk = math.gcd(count, 512)

    def operate(field):
        masked = mask * field

        def one_block(start):
            rows = lax.dynamic_slice_in_dim(scaled, start, rowblk, 0)
            return jnp.dot(matern(rows, scaled), masked, precision=lax.Precision.HIGHEST, preferred_element_type=jnp.float32)
        starts = (jnp.arange(count // rowblk) * rowblk).astype(jnp.int32)
        mixed = lax.map(one_block, starts).reshape(count, -1)
        timed = jnp.dot(mixed, time_kernel, precision=lax.Precision.HIGHEST, preferred_element_type=jnp.float32)
        return mask * timed + noise[:, None] * field
    residual = mask * targets
    direction = residual
    solution_field = jnp.zeros_like(residual)
    norm_now = jnp.sum(residual * residual)
    for step in range(ITERS):
        image = operate(direction)
        alpha = norm_now / jnp.sum(direction * image)
        solution_field = solution_field + alpha * direction
        residual = residual - alpha * image
        norm_next = jnp.sum(residual * residual)
        direction = residual + norm_next / norm_now * direction
        norm_now = norm_next
    return (solution_field, residual)
```

```python
import jax
import jax.numpy as jnp
from jax import lax
from jax.sharding import PartitionSpec as P

HIGH = lax.Precision.HIGH
HIGHEST = lax.Precision.HIGHEST


def dot(left, right, precision=HIGH):
    return jnp.dot(left, right, precision=precision, preferred_element_type=jnp.float32)


def partners(count, offset):
    return [(index, index ^ offset) for index in range(count)]


def gather_cfg(block, count):
    own = [block] + [lax.ppermute(block, "cfg", partners(count, d)) for d in range(2, count, 2)]
    other = [lax.ppermute(piece, "cfg", partners(count, 1)) for piece in own]
    return [piece for pair in zip(own, other) for piece in pair]


def total(value, count):
    sent = jnp.broadcast_to(value[None, :, None], (count, 8, 128))
    got = lax.all_to_all(sent, ("cfg", "tm"), 0, 0, tiled=True)
    return jnp.sum(got, axis=0)[:, 0]


def matern(left, right_t):
    cross = dot(left, right_t, HIGHEST)
    dist2 = (
        jnp.sum(left * left, axis=1)[:, None]
        + jnp.sum(right_t * right_t, axis=0)[None, :]
        - 2.0 * cross
    )
    scaled_dist = jnp.sqrt(3.0) * jnp.sqrt(jnp.maximum(dist2, 0.0))
    return (1.0 + scaled_dist) * jnp.exp(-scaled_dist)


def solution(mesh):
    cfg, tm = mesh.shape["cfg"], mesh.shape["tm"]
    everyone = cfg * tm

    def body(targets, features, inv_scales, noise, time_kernel, block_mask):
        mask = block_mask.astype(jnp.float32)
        ridge = noise[:, None]
        scaled = features * inv_scales[None, :]
        every_t = jnp.concatenate(gather_cfg(scaled.T, cfg), axis=1)
        residual = mask * targets
        steps = time_kernel.T

        def over_time(field):
            rows = lax.all_gather(field, "tm", axis=0)
            mixed = dot(rows[0], steps[: field.shape[1]])
            for part in range(1, tm):
                mixed = mixed + dot(rows[part], steps[part * field.shape[1] : (part + 1) * field.shape[1]])
            return mixed

        timed = over_time(residual)
        tile = matern(scaled, every_t)

        def over_cfg(field):
            return dot(tile, jnp.concatenate(gather_cfg(field, cfg), axis=0))

        image = mask * over_cfg(timed) + ridge * residual
        second = mask * over_cfg(over_time(image)) + ridge * image
        parts = jnp.stack(
            [
                jnp.sum(residual * residual),
                jnp.sum(residual * image),
                jnp.sum(image * image),
                jnp.sum(image * second),
            ]
            + [jnp.float32(0.0)] * 4
        )
        sums = total(parts, everyone)
        alpha = sums[0] / sums[1]
        norm = sums[0] - 2.0 * alpha * sums[1] + alpha * alpha * sums[2]
        ratio = norm / sums[0]
        keep = 1.0 + ratio
        curv = keep * keep * sums[1] - 2.0 * keep * alpha * sums[2] + alpha * alpha * sums[3]
        beta = norm / curv
        direction = keep * residual - alpha * image
        solution_field = alpha * residual + beta * direction
        left = residual - alpha * image - beta * (keep * image - alpha * second)
        return (solution_field, left)

    return jax.shard_map(
        body,
        mesh=mesh,
        in_specs=(P("cfg", "tm"), P("cfg", None), P(), P("cfg"), P("tm", None), P("cfg", "tm")),
        out_specs=(P("cfg", "tm"), P("cfg", "tm")),
        check_vma=False,
    )
```

```python
import functools

import jax
import jax.numpy as jnp
from jax import lax
from jax.experimental import pallas as pl
from jax.experimental.pallas import tpu as pltpu
from jax.sharding import PartitionSpec as P

HIGH = lax.Precision.HIGH
HIGHEST = lax.Precision.HIGHEST
VMEM = pl.BlockSpec(memory_space=pltpu.VMEM)
SMALL = pltpu.CompilerParams(vmem_limit_bytes=16 * 1024 * 1024)


def dot(left, right, precision=HIGH):
    return jnp.dot(left, right, precision=precision, preferred_element_type=jnp.float32)


def partners(count, offset):
    return [(index, index ^ offset) for index in range(count)]


def gather_cfg(block, count):
    own = [block] + [lax.ppermute(block, "cfg", partners(count, d)) for d in range(2, count, 2)]
    other = [lax.ppermute(piece, "cfg", partners(count, 1)) for piece in own]
    return [piece for pair in zip(own, other) for piece in pair]


def gather_tm(block, count):
    return [block] + [lax.ppermute(block, "tm", partners(count, d)) for d in range(1, count)]


def matern(left, right_t):
    cross = dot(left, right_t, HIGHEST)
    dist2 = (
        jnp.sum(left * left, axis=1)[:, None]
        + jnp.sum(right_t * right_t, axis=0)[None, :]
        - 2.0 * cross
    )
    scaled_dist = jnp.sqrt(3.0) * jnp.sqrt(jnp.maximum(dist2, 0.0))
    return (1.0 + scaled_dist) * jnp.exp(-scaled_dist)


def column(row):
    return jnp.transpose(jnp.broadcast_to(row, (8, row.shape[1])))[:, :1]


def total_of(left, right):
    product = left * right
    return jnp.sum(jnp.sum(product, axis=0, keepdims=True), axis=1, keepdims=True)


def moments_kernel(mixed_ref, mask_ref, noise_ref, image_ref, residual_ref, second_ref, parts_ref):
    image, residual = image_ref[...], residual_ref[...]
    second = column(mask_ref[...]) * mixed_ref[...] + column(noise_ref[...]) * image
    second_ref[...] = second
    place = lax.broadcasted_iota(jnp.int32, parts_ref.shape[1:], 0)
    parts = jnp.zeros(parts_ref.shape[1:], jnp.float32)
    for at, pair in enumerate([(residual, residual), (residual, image), (image, image), (image, second)]):
        parts = jnp.where(place == at, total_of(*pair), parts)
    parts_ref[...] = jnp.broadcast_to(parts[None], parts_ref.shape)


def finish_kernel(parts_ref, residual_ref, image_ref, second_ref, field_ref, left_ref):
    sums = jnp.sum(parts_ref[...], axis=0)
    norm0, first, square, third = (sums[at : at + 1] for at in range(4))
    alpha = norm0 / first
    norm1 = norm0 - 2.0 * alpha * first + alpha * alpha * square
    keep = 1.0 + norm1 / norm0
    curv = keep * keep * first - 2.0 * keep * alpha * square + alpha * alpha * third
    beta = norm1 / curv
    residual, image = residual_ref[...], image_ref[...]
    field_ref[...] = (alpha + beta * keep) * residual - (beta * alpha) * image
    left_ref[...] = residual - (alpha + beta * keep) * image + (beta * alpha) * second_ref[...]


def solution(mesh):
    cfg, tm = mesh.shape["cfg"], mesh.shape["tm"]
    everyone = cfg * tm

    def body(targets, features, inv_scales, noise, time_kernel, block_mask):
        rows, width = targets.shape
        layer = lax.axis_index("tm")
        mask = block_mask.astype(jnp.float32)
        ridge = noise[:, None]
        residual = mask * targets
        scaled = features * inv_scales[None, :]
        every_t = gather_cfg(scaled.T, cfg)
        steps = jnp.concatenate(
            [lax.dynamic_slice(time_kernel, (0, (layer ^ d) * width), (width, width)) for d in range(tm)], axis=1
        )

        def over_time(field):
            whole = jnp.concatenate(gather_tm(field, tm), axis=1)
            return lax.dot_general(
                whole, steps, (((1,), (1,)), ((), ())), precision=HIGH, preferred_element_type=jnp.float32
            )

        timed = over_time(residual)
        tile = matern(scaled, jnp.concatenate(every_t, axis=1))

        def over_cfg(field):
            return dot(tile, jnp.concatenate(gather_cfg(field, cfg), axis=0))

        image = mask * over_cfg(timed) + ridge * residual
        mixed = over_cfg(over_time(image))
        block = jax.ShapeDtypeStruct((rows, width), jnp.float32)
        second, parts = pl.pallas_call(
            moments_kernel,
            out_shape=(block, jax.ShapeDtypeStruct((everyone, 8, width), jnp.float32)),
            in_specs=[VMEM] * 5,
            out_specs=(VMEM, VMEM),
            compiler_params=SMALL,
            name="moments",
        )(mixed, mask.reshape(1, rows), noise.reshape(1, rows), image, residual)
        parts = lax.all_to_all(parts, ("cfg", "tm"), 0, 0, tiled=True)
        return pl.pallas_call(
            finish_kernel,
            out_shape=(block, block),
            in_specs=[VMEM] * 4,
            out_specs=(VMEM, VMEM),
            compiler_params=SMALL,
            name="finish",
        )(parts, residual, image, second)

    return jax.shard_map(
        body,
        mesh=mesh,
        in_specs=(P("cfg", "tm"), P("cfg", None), P(), P("cfg"), P("tm", None), P("cfg", "tm")),
        out_specs=(P("cfg", "tm"), P("cfg", "tm")),
        check_vma=False,
    )
```

```python
import math

import jax
import jax.numpy as jnp
from jax import lax
from jax.experimental import pallas as pl
from jax.experimental.pallas import tpu as pltpu
from jax.sharding import PartitionSpec as P

HBM = pl.BlockSpec(memory_space=pltpu.HBM)
VMEM = pl.BlockSpec(memory_space=pltpu.VMEM)
SMEM = pl.BlockSpec(memory_space=pltpu.SMEM)
F32, BF16 = jnp.float32, jnp.bfloat16
LIMIT = 62
LOG2E, LN2 = math.log2(math.e), math.log(2.0)


def partners(axis, offset):
    return [(index, index ^ offset) for index in range(lax.axis_size(axis))]


def gather_cfg(block, count, meanwhile=None):
    own = [block] + [lax.ppermute(block, "cfg", partners("cfg", d)) for d in range(2, count, 2)]
    if meanwhile is not None:
        extra = meanwhile(block)
        *extra, own[-1] = lax.optimization_barrier((*extra, own[-1]))
    other = [lax.ppermute(piece, "cfg", partners("cfg", 1)) for piece in own]
    pieces = [piece for pair in zip(own, other) for piece in pair]
    return pieces if meanwhile is None else (pieces, extra)


def gather_tm(block, count):
    return [block] + [lax.ppermute(block, "tm", partners("tm", d)) for d in range(1, count)]


def call(kernel, name, outs, *args, scalars=0, scratch=(), limit=24, space=VMEM, cost=None):
    return pl.pallas_call(
        kernel,
        out_shape=outs,
        in_specs=[SMEM] * scalars + [space] * (len(args) - scalars),
        cost_estimate=cost,
        out_specs=jax.tree.map(lambda _: VMEM, outs),
        scratch_shapes=list(scratch),
        compiler_params=pltpu.CompilerParams(vmem_limit_bytes=limit * 1024 * 1024),
        name=name,
    )(*args)


def split(value):
    high = value.astype(BF16)
    return high, (value - high.astype(F32)).astype(BF16)


def mul(left, right):
    return jnp.dot(left, right, preferred_element_type=F32)


def mul3(left, right):
    return mul(left[0], right[0]) + (mul(left[0], right[1]) + mul(left[1], right[0]))


def column(row):
    size = min(128, row.shape[1])
    same = lax.broadcasted_iota(jnp.int32, (size, size), 0) == lax.broadcasted_iota(jnp.int32, (size, size), 1)
    return jnp.concatenate(
        [
            jnp.sum(jnp.where(same, row[:, at : at + size], 0.0), axis=1, keepdims=True)
            for at in range(0, row.shape[1], size)
        ],
        axis=0,
    )


def total_of(left, right):
    return jnp.sum(jnp.sum(left * right, axis=0, keepdims=True), axis=1, keepdims=True)


def fetch(pairs, sems):
    copies = [pltpu.make_async_copy(src, dst, sems.at[at]) for at, (src, dst) in enumerate(pairs)]
    for copy in copies:
        copy.start()
    for copy in copies:
        copy.wait()


def begin_kernel(targets_hbm, features_hbm, scales_hbm, mask_hbm, residual_ref, scaled_ref, flag_ref, *rest):
    targets_ref, features_ref, scales_ref, mask_ref, sems = rest
    fetch(
        [(mask_hbm, mask_ref), (targets_hbm, targets_ref), (scales_hbm, scales_ref), (features_hbm, features_ref)], sems
    )
    flag_ref[...] = mask_ref[...].astype(F32)
    residual_ref[...] = column(flag_ref[...]) * targets_ref[...]
    scaled_ref[...] = column(scales_ref[...] * (math.sqrt(3.0) * LOG2E)) * features_ref[...]


def split3(value):
    high, rest = value.astype(BF16), value
    rest = rest - high.astype(F32)
    middle = rest.astype(BF16)
    return high, middle, (rest - middle.astype(F32)).astype(BF16)


def mul_tile(high, low, field):
    width = field.shape[1]
    field_high, field_low = split(field)
    both = mul(high, jnp.concatenate([field_high, field_low], axis=1))
    return both[:, :width] + (both[:, width:] + mul(low, field_high))


def layers_kernel(place_ref, steps_ref, mask_ref, noise_ref, _, high_ref, low_ref, flag_ref, ridge_ref):
    width = steps_ref.shape[0]
    for offset in range(steps_ref.shape[1] // width):
        at = pl.ds(offset * width, width)
        high_ref[:, at], low_ref[:, at] = split(
            steps_ref[:, pl.ds(pl.multiple_of((place_ref[1] ^ offset) * width, width), width)]
        )
    flag_ref[...] = column(mask_ref[...])
    ridge_ref[...] = column(noise_ref[...])


def tile_kernel(place_ref, every_ref, _, high_ref, low_ref):
    rows = high_ref.shape[0]
    left = jnp.transpose(every_ref[place_ref[0]])
    left_sq = jnp.sum(left * left, axis=1, keepdims=True)
    high, middle, low = split3(-2.0 * left)
    left = jnp.concatenate([high, high, middle, middle, high, low], axis=1)
    for offset in range(every_ref.shape[0]):
        right = every_ref[place_ref[0] ^ offset]
        right_sq = jnp.sum(right * right, axis=0, keepdims=True)
        high, middle, low = split3(right)
        cross = mul(left, jnp.concatenate([high, middle, high, middle, low, high], axis=0))
        dist2 = jnp.maximum(left_sq + right_sq + cross, 1e-30)
        dist = dist2 * lax.rsqrt(dist2)
        high, low = split((1.0 + LN2 * dist) * jnp.exp2(-dist))
        high_ref[:, pl.ds(offset * rows, rows)] = high
        low_ref[:, pl.ds(offset * rows, rows)] = low


def mul_t(left, right):
    return lax.dot_general(left, right, (((1,), (1,)), ((), ())), preferred_element_type=F32)


def steps_kernel(*refs):
    pieces, (high_ref, low_ref, out_ref) = refs[:-3], refs[-3:]
    field = split(jnp.concatenate([piece[...] for piece in pieces], axis=1))
    out_ref[...] = mul_t(field[0], high_ref[...]) + (mul_t(field[0], low_ref[...]) + mul_t(field[1], high_ref[...]))


def image_of(refs):
    pieces, (high_ref, low_ref, flag_ref, ridge_ref, field_ref) = refs[:-5], refs[-5:]
    mixed = mul_tile(high_ref[...], low_ref[...], jnp.concatenate([piece[...] for piece in pieces], axis=0))
    return flag_ref[...] * mixed + ridge_ref[...] * field_ref[...]


def image_kernel(*refs):
    refs[-1][...] = image_of(refs[:-1])


def moments_kernel(*refs):
    image_ref, residual_ref, second_ref, parts_ref = refs[-4:]
    second = image_of(refs[:-3])
    image, residual = image_ref[...], residual_ref[...]
    second_ref[...] = second
    lane = lax.broadcasted_iota(jnp.int32, parts_ref.shape[1:], 1)
    parts = jnp.zeros(parts_ref.shape[1:], F32)
    for at, pair in enumerate([(residual, residual), (residual, image), (image, image), (image, second)]):
        parts = jnp.where(lane == at, total_of(*pair), parts)
    parts_ref[...] = jnp.broadcast_to(parts[None], parts_ref.shape)


def finish_kernel(parts_ref, residual_ref, image_ref, second_ref, field_ref, left_ref):
    sums = jnp.sum(parts_ref[...], axis=0)
    norm0, first, square, third = (sums[:, at : at + 1] for at in range(4))
    alpha = norm0 / first
    norm1 = norm0 - 2.0 * alpha * first + alpha * alpha * square
    keep = 1.0 + norm1 / norm0
    curv = keep * keep * first - 2.0 * keep * alpha * square + alpha * alpha * third
    beta = norm1 / curv
    residual, image = residual_ref[...], image_ref[...]
    field_ref[...] = (alpha + beta * keep) * residual - (beta * alpha) * image
    left_ref[...] = residual - (alpha + beta * keep) * image + (beta * alpha) * second_ref[...]


def solution(mesh):
    cfg, tm = mesh.shape["cfg"], mesh.shape["tm"]

    def body(targets, features, inv_scales, noise, time_kernel, block_mask):
        rows, width = targets.shape
        count = features.shape[1]
        place = jnp.stack([lax.axis_index("cfg"), lax.axis_index("tm")])
        mask = block_mask.reshape(1, rows)

        def shape(*size, kind=F32):
            return jax.ShapeDtypeStruct(size, kind)

        block = shape(rows, width)
        residual, scaled, flag = call(
            begin_kernel,
            "begin",
            (block, shape(count, rows), shape(1, rows)),
            targets, features.T, inv_scales.reshape(1, count), mask,
            space=HBM,
            scratch=[
                pltpu.VMEM((rows, width), F32),
                pltpu.VMEM((count, rows), F32),
                pltpu.VMEM((1, count), F32),
                pltpu.VMEM((1, rows), mask.dtype),
                pltpu.SemaphoreType.DMA((4,)),
            ],
            limit=LIMIT,
        )

        every = lax.all_gather(scaled, "cfg")
        half, steps, col = shape(rows, cfg * rows, kind=BF16), shape(width, tm * width, kind=BF16), shape(rows, 1)
        steps_high, steps_low, flag, ridge = call(
            layers_kernel,
            "layers",
            (steps, steps, col, col),
            place, time_kernel, flag, noise.reshape(1, rows), every,
            scalars=1,
        )

        def over_time(field):
            return call(steps_kernel, "steps", block, *gather_tm(field, tm), steps_high, steps_low)

        fields, (high, low) = gather_cfg(
            over_time(residual),
            cfg,
            lambda timed: call(tile_kernel, "tile", (half, half), place, every, timed, scalars=1),
        )
        image = call(image_kernel, "image", block, *fields, high, low, flag, ridge, residual)
        second, sums = call(
            moments_kernel,
            "moments",
            (block, shape(cfg * tm, 1, width)),
            *gather_cfg(over_time(image), cfg), high, low, flag, ridge, image, residual,
        )
        sums = lax.all_to_all(sums, ("cfg", "tm"), 0, 0, tiled=True)
        return call(finish_kernel, "finish", (block, block), sums, residual, image, second)

    return jax.shard_map(
        body,
        mesh=mesh,
        in_specs=(P("cfg", "tm"), P("cfg", None), P(), P("cfg"), P("tm", None), P("cfg", "tm")),
        out_specs=(P("cfg", "tm"), P("cfg", "tm")),
        check_vma=False,
    )
```

```python
import math

import jax
import jax.numpy as jnp
from jax import lax
from jax.experimental import pallas as pl
from jax.experimental.pallas import tpu as pltpu
from jax.sharding import PartitionSpec as P

HBM = pl.BlockSpec(memory_space=pltpu.HBM)
VMEM = pl.BlockSpec(memory_space=pltpu.VMEM)
SMEM = pl.BlockSpec(memory_space=pltpu.SMEM)
F32, BF16 = jnp.float32, jnp.bfloat16
LIMIT = 62
LOG2E, LN2 = math.log2(math.e), math.log(2.0)


def partners(axis, offset):
    return [(index, index ^ offset) for index in range(lax.axis_size(axis))]


def gather_cfg(block, count, meanwhile=None):
    own = [block] + [lax.ppermute(block, "cfg", partners("cfg", d)) for d in range(2, count, 2)]
    if meanwhile is not None:
        extra = meanwhile(block)
        *extra, own[-1] = lax.optimization_barrier((*extra, own[-1]))
    other = [lax.ppermute(piece, "cfg", partners("cfg", 1)) for piece in own]
    return own + other if meanwhile is None else (own + other, extra)


def gather_tm(block, count):
    return [block] + [lax.ppermute(block, "tm", partners("tm", d)) for d in range(1, count)]


def call(kernel, name, outs, *args, scalars=0, scratch=(), limit=24, space=VMEM, cost=None):
    return pl.pallas_call(
        kernel,
        out_shape=outs,
        in_specs=[SMEM] * scalars + [space] * (len(args) - scalars),
        cost_estimate=cost,
        out_specs=jax.tree.map(lambda _: VMEM, outs),
        scratch_shapes=list(scratch),
        compiler_params=pltpu.CompilerParams(vmem_limit_bytes=limit * 1024 * 1024),
        name=name,
    )(*args)


def split(value):
    high = value.astype(BF16)
    return high, (value - high.astype(F32)).astype(BF16)


def mul(left, right):
    return jnp.dot(left, right, preferred_element_type=F32)


def mul3(left, right):
    return mul(left[0], right[0]) + (mul(left[0], right[1]) + mul(left[1], right[0]))


def column(row):
    size = min(128, row.shape[1])
    same = lax.broadcasted_iota(jnp.int32, (size, size), 0) == lax.broadcasted_iota(jnp.int32, (size, size), 1)
    return jnp.concatenate(
        [
            jnp.sum(jnp.where(same, row[:, at : at + size], 0.0), axis=1, keepdims=True)
            for at in range(0, row.shape[1], size)
        ],
        axis=0,
    )


def total_of(left, right):
    return jnp.sum(jnp.sum(left * right, axis=0, keepdims=True), axis=1, keepdims=True)


def fetch(pairs, sems):
    copies = [pltpu.make_async_copy(src, dst, sems.at[at]) for at, (src, dst) in enumerate(pairs)]
    for copy in copies:
        copy.start()
    for copy in copies:
        copy.wait()


def begin_kernel(targets_hbm, features_hbm, scales_hbm, mask_hbm, residual_ref, scaled_ref, flag_ref, *rest):
    targets_ref, features_ref, scales_ref, mask_ref, sems = rest
    fetch(
        [(mask_hbm, mask_ref), (targets_hbm, targets_ref), (scales_hbm, scales_ref), (features_hbm, features_ref)], sems
    )
    flag_ref[...] = mask_ref[...].astype(F32)
    residual_ref[...] = column(flag_ref[...]) * targets_ref[...]
    scaled_ref[...] = column(scales_ref[...] * (math.sqrt(3.0) * LOG2E)) * features_ref[...]


def split3(value):
    high, rest = value.astype(BF16), value
    rest = rest - high.astype(F32)
    middle = rest.astype(BF16)
    return high, middle, (rest - middle.astype(F32)).astype(BF16)


def mul_tile(high, low, field):
    width = field.shape[1]
    field_high, field_low = split(field)
    both = mul(high, jnp.concatenate([field_high, field_low], axis=1))
    return both[:, :width] + (both[:, width:] + mul(low, field_high))


def layers_kernel(place_ref, steps_ref, mask_ref, noise_ref, high_ref, low_ref, flag_ref, ridge_ref):
    width = steps_ref.shape[0]
    for offset in range(steps_ref.shape[1] // width):
        at = pl.ds(offset * width, width)
        high_ref[:, at], low_ref[:, at] = split(
            steps_ref[:, pl.ds(pl.multiple_of((place_ref[0] ^ offset) * width, width), width)]
        )
    flag_ref[...] = column(mask_ref[...])
    ridge_ref[...] = column(noise_ref[...])


def tile_kernel(*refs):
    pieces, (_, high_ref, low_ref) = refs[:-3], refs[-3:]
    rows = high_ref.shape[0]
    left = jnp.transpose(pieces[0][...])
    left_sq = jnp.sum(left * left, axis=1, keepdims=True)
    high, middle, low = split3(-2.0 * left)
    left = jnp.concatenate([high, high, middle, middle, high, low], axis=1)
    for at, piece in enumerate(pieces):
        right = piece[...]
        right_sq = jnp.sum(right * right, axis=0, keepdims=True)
        high, middle, low = split3(right)
        cross = mul(left, jnp.concatenate([high, middle, high, middle, low, high], axis=0))
        dist2 = jnp.maximum(left_sq + right_sq + cross, 1e-30)
        dist = dist2 * lax.rsqrt(dist2)
        high, low = split((1.0 + LN2 * dist) * jnp.exp2(-dist))
        high_ref[:, pl.ds(at * rows, rows)] = high
        low_ref[:, pl.ds(at * rows, rows)] = low


def mul_t(left, right):
    return lax.dot_general(left, right, (((1,), (1,)), ((), ())), preferred_element_type=F32)


def steps_kernel(*refs):
    pieces, (high_ref, low_ref, out_ref) = refs[:-3], refs[-3:]
    field = split(jnp.concatenate([piece[...] for piece in pieces], axis=1))
    out_ref[...] = mul_t(field[0], high_ref[...]) + (mul_t(field[0], low_ref[...]) + mul_t(field[1], high_ref[...]))


def partial_kernel(*refs):
    pieces, (high_ref, low_ref, out_ref) = refs[:-3], refs[-3:]
    field = jnp.concatenate([piece[...] for piece in pieces], axis=0)
    at = pl.ds(0, field.shape[0])
    out_ref[...] = mul_tile(high_ref[:, at], low_ref[:, at], field)


def image_of(refs):
    pieces, (partial_ref, high_ref, low_ref, flag_ref, ridge_ref, field_ref) = refs[:-6], refs[-6:]
    field = jnp.concatenate([piece[...] for piece in pieces], axis=0)
    at = pl.ds(high_ref.shape[1] - field.shape[0], field.shape[0])
    mixed = partial_ref[...] + mul_tile(high_ref[:, at], low_ref[:, at], field)
    return flag_ref[...] * mixed + ridge_ref[...] * field_ref[...]


def image_kernel(*refs):
    refs[-1][...] = image_of(refs[:-1])


def moments_kernel(*refs):
    image_ref, residual_ref, second_ref, parts_ref = refs[-4:]
    second = image_of(refs[:-3])
    image, residual = image_ref[...], residual_ref[...]
    second_ref[...] = second
    lane = lax.broadcasted_iota(jnp.int32, parts_ref.shape[1:], 1)
    parts = jnp.zeros(parts_ref.shape[1:], F32)
    for at, pair in enumerate([(residual, residual), (residual, image), (image, image), (image, second)]):
        parts = jnp.where(lane == at, total_of(*pair), parts)
    parts_ref[...] = jnp.broadcast_to(parts[None], parts_ref.shape)


def finish_kernel(parts_ref, residual_ref, image_ref, second_ref, field_ref, left_ref):
    sums = jnp.sum(parts_ref[...], axis=0)
    norm0, first, square, third = (sums[:, at : at + 1] for at in range(4))
    alpha = norm0 / first
    norm1 = norm0 - 2.0 * alpha * first + alpha * alpha * square
    keep = 1.0 + norm1 / norm0
    curv = keep * keep * first - 2.0 * keep * alpha * square + alpha * alpha * third
    beta = norm1 / curv
    residual, image = residual_ref[...], image_ref[...]
    field_ref[...] = (alpha + beta * keep) * residual - (beta * alpha) * image
    left_ref[...] = residual - (alpha + beta * keep) * image + (beta * alpha) * second_ref[...]


def solution(mesh):
    cfg, tm = mesh.shape["cfg"], mesh.shape["tm"]

    def body(targets, features, inv_scales, noise, time_kernel, block_mask):
        rows, width = targets.shape
        count = features.shape[1]
        place = lax.axis_index("tm").reshape(1)
        mask = block_mask.reshape(1, rows)

        def shape(*size, kind=F32):
            return jax.ShapeDtypeStruct(size, kind)

        block = shape(rows, width)
        residual, scaled, flag = call(
            begin_kernel,
            "begin",
            (pltpu.VMEM((rows, width), F32), pltpu.VMEM((count, rows), F32), pltpu.VMEM((1, rows), F32)),
            targets, features.T, inv_scales.reshape(1, count), mask,
            space=HBM,
            scratch=[
                pltpu.VMEM((rows, width), F32),
                pltpu.VMEM((count, rows), F32),
                pltpu.VMEM((1, count), F32),
                pltpu.VMEM((1, rows), mask.dtype),
                pltpu.SemaphoreType.DMA((4,)),
            ],
            limit=LIMIT,
        )

        half, steps, col = shape(rows, cfg * rows, kind=BF16), shape(width, tm * width, kind=BF16), shape(rows, 1)
        steps_high, steps_low, flag, ridge = call(
            layers_kernel,
            "layers",
            (steps, steps, col, col),
            place, time_kernel, flag, noise.reshape(1, rows),
            scalars=1,
        )
        residuals, every = lax.optimization_barrier((gather_tm(residual, tm), gather_cfg(scaled, cfg)))

        def over_time(pieces):
            return call(steps_kernel, "steps", block, *pieces, steps_high, steps_low)

        fields, (high, low) = gather_cfg(
            over_time(residuals), cfg, lambda timed: call(tile_kernel, "tile", (half, half), *every, timed)
        )

        def over_cfg(pieces):
            early = len(pieces) // 2 + 1
            partial = call(partial_kernel, "partial", block, *pieces[:early], high, low)
            return [*pieces[early:], partial, high, low, flag, ridge]

        image = call(image_kernel, "image", block, *over_cfg(fields), residual)
        second, sums = call(
            moments_kernel,
            "moments",
            (block, shape(cfg * tm, 1, width)),
            *over_cfg(gather_cfg(over_time(gather_tm(image, tm)), cfg)), image, residual,
        )
        sums = lax.all_to_all(sums, ("cfg", "tm"), 0, 0, tiled=True)
        return call(finish_kernel, "finish", (block, block), sums, residual, image, second)

    return jax.shard_map(
        body,
        mesh=mesh,
        in_specs=(P("cfg", "tm"), P("cfg", None), P(), P("cfg"), P("tm", None), P("cfg", "tm")),
        out_specs=(P("cfg", "tm"), P("cfg", "tm")),
        check_vma=False,
    )
```

```python
import functools
import math

import jax
import jax.numpy as jnp
from jax import lax
from jax.experimental import pallas as pl
from jax.experimental.pallas import tpu as pltpu
from jax.sharding import PartitionSpec as P

HBM = pl.BlockSpec(memory_space=pltpu.HBM)
ANY = pl.BlockSpec(memory_space=pl.ANY)
VMEM = pl.BlockSpec(memory_space=pltpu.VMEM)
SMEM = pl.BlockSpec(memory_space=pltpu.SMEM)
F32, BF16 = jnp.float32, jnp.bfloat16
LIMIT = 62
LOG2E, LN2 = math.log2(math.e), math.log(2.0)


def partners(axis, offset):
    return [(index, index ^ offset) for index in range(lax.axis_size(axis))]


def far_cfg(block):
    return [block] + [lax.ppermute(block, "cfg", partners("cfg", d)) for d in range(2, lax.axis_size("cfg"), 2)]


def near_cfg(block):
    return lax.ppermute(block, "cfg", partners("cfg", 1))


def offsets_tm(layers):
    return [0] + [d for d in (layers - 1, *range(1, layers - 1)) if d]


def gather_tm(block):
    return [block] + [lax.ppermute(block, "tm", partners("tm", d)) for d in offsets_tm(lax.axis_size("tm"))[1:]]


def call(kernel, name, outs, *args, scalars=0, unread=0, scratch=(), limit=24, space=VMEM, cost=None):
    return pl.pallas_call(
        kernel,
        out_shape=outs,
        in_specs=[SMEM] * scalars + [space] * (len(args) - scalars - unread) + [ANY] * unread,
        cost_estimate=cost,
        out_specs=jax.tree.map(lambda _: VMEM, outs),
        scratch_shapes=list(scratch),
        compiler_params=pltpu.CompilerParams(vmem_limit_bytes=limit * 1024 * 1024),
        name=name,
    )(*args)


def split(value):
    high = value.astype(BF16)
    return high, (value - high.astype(F32)).astype(BF16)


def mul(left, right):
    return jnp.dot(left, right, preferred_element_type=F32)


def mul3(left, right):
    return mul(left[0], right[0]) + (mul(left[0], right[1]) + mul(left[1], right[0]))


def column(row):
    size = min(128, row.shape[1])
    same = lax.broadcasted_iota(jnp.int32, (size, size), 0) == lax.broadcasted_iota(jnp.int32, (size, size), 1)
    return jnp.concatenate(
        [
            jnp.sum(jnp.where(same, row[:, at : at + size], 0.0), axis=1, keepdims=True)
            for at in range(0, row.shape[1], size)
        ],
        axis=0,
    )


def total_of(left, right):
    return jnp.sum(jnp.sum(left * right, axis=0, keepdims=True), axis=1, keepdims=True)


def fetch(pairs, sems):
    copies = [pltpu.make_async_copy(src, dst, sems.at[at]) for at, (src, dst) in enumerate(pairs)]
    for copy in copies:
        copy.start()
    for copy in copies:
        copy.wait()


def begin_kernel(targets_hbm, features_hbm, scales_hbm, mask_hbm, noise_hbm, residual_ref, scaled_ref, *rest):
    flag_ref, ridge_ref, targets_ref, features_ref, scales_ref, mask_ref, sems = rest
    fetch(
        [
            (mask_hbm, mask_ref),
            (targets_hbm, targets_ref),
            (scales_hbm, scales_ref),
            (features_hbm, features_ref),
            (noise_hbm, ridge_ref),
        ],
        sems,
    )
    flag_ref[...] = mask_ref[...].astype(F32)
    residual_ref[...] = column(flag_ref[...]) * targets_ref[...]
    scaled_ref[...] = column(scales_ref[...] * (math.sqrt(3.0) * LOG2E)) * features_ref[...]


def split3(value):
    high, rest = value.astype(BF16), value
    rest = rest - high.astype(F32)
    middle = rest.astype(BF16)
    return high, middle, (rest - middle.astype(F32)).astype(BF16)


def mul_tile(high, low, field):
    width = field.shape[1]
    field_high, field_low = split(field)
    both = mul(high, jnp.concatenate([field_high, field_low], axis=1))
    return both[:, :width] + (both[:, width:] + mul(low, field_high))


def layers_kernel(layer_ref, steps_ref, _, __, high_ref, low_ref):
    width = steps_ref.shape[0]
    for place, offset in enumerate(offsets_tm(steps_ref.shape[1] // width)):
        at = pl.ds(place * width, width)
        high_ref[:, at], low_ref[:, at] = split(
            steps_ref[:, pl.ds(pl.multiple_of((layer_ref[0] ^ offset) * width, width), width)]
        )


def tile_kernel(pair_ref, near_ref, every_ref, mask_ref, noise_ref, _, high_ref, low_ref, flag_ref, ridge_ref):
    flag_ref[...] = column(mask_ref[...])
    ridge_ref[...] = column(noise_ref[...])
    rows, pair = every_ref.shape[2], pair_ref[0]
    pieces = [every_ref.at[pair ^ offset] for offset in range(every_ref.shape[0])]
    left = jnp.transpose(jnp.concatenate([pieces[0][...], near_ref[...]], axis=1))
    left_sq = jnp.sum(left * left, axis=1, keepdims=True)
    high, middle, low = split3(-2.0 * left)
    left = jnp.concatenate([high, high, middle, middle, high, low], axis=1)
    for at, piece in enumerate(pieces):
        right = piece[...]
        right_sq = jnp.sum(right * right, axis=0, keepdims=True)
        high, middle, low = split3(right)
        cross = mul(left, jnp.concatenate([high, middle, high, middle, low, high], axis=0))
        dist2 = jnp.maximum(left_sq + right_sq + cross, 1e-30)
        dist = dist2 * lax.rsqrt(dist2)
        high, low = split((1.0 + LN2 * dist) * jnp.exp2(-dist))
        high_ref[:, pl.ds(at * rows, rows)] = high
        low_ref[:, pl.ds(at * rows, rows)] = low


def mul_t(left, right):
    return lax.dot_general(left, right, (((1,), (1,)), ((), ())), preferred_element_type=F32)


def steps_kernel(*refs):
    pieces, (high_ref, low_ref, out_ref) = refs[:-3], refs[-3:]
    field = split(jnp.concatenate([piece[...] for piece in pieces], axis=1))
    out_ref[...] = mul_t(field[0], high_ref[...]) + (mul_t(field[0], low_ref[...]) + mul_t(field[1], high_ref[...]))


def share(at, pieces, high_ref, low_ref):
    rows = pieces[0].shape[0]
    high, low = (jnp.concatenate([ref[:, pl.ds(place * rows, rows)] for place in at], axis=1) for ref in (high_ref, low_ref))
    return mul_tile(high, low, jnp.concatenate([piece[...] for piece in pieces], axis=0))


def early_kernel(at, *refs):
    pieces, (high_ref, low_ref, out_ref) = refs[:-3], refs[-3:]
    out_ref[...] = share(at, pieces, high_ref, low_ref)


def late_kernel(at, *refs):
    pieces, (early_ref, high_ref, low_ref, own_ref, near_ref) = refs[:-5], refs[-5:]
    mixed = early_ref[...] + share(at, pieces, high_ref, low_ref)
    own_ref[...] = mixed[: own_ref.shape[0]]
    near_ref[...] = mixed[own_ref.shape[0] :]


def image_of(own_ref, near_ref, flag_ref, ridge_ref, field_ref):
    return flag_ref[...] * (own_ref[...] + near_ref[...]) + ridge_ref[...] * field_ref[...]


def image_kernel(*refs):
    refs[-1][...] = image_of(*refs[:-1])


def moments_kernel(*refs):
    image_ref, residual_ref, second_ref, parts_ref = refs[-4:]
    second = image_of(*refs[:-3])
    image, residual = image_ref[...], residual_ref[...]
    second_ref[...] = second
    lane = lax.broadcasted_iota(jnp.int32, parts_ref.shape[1:], 1)
    parts = jnp.zeros(parts_ref.shape[1:], F32)
    for at, pair in enumerate([(residual, residual), (residual, image), (image, image), (image, second)]):
        parts = jnp.where(lane == at, total_of(*pair), parts)
    parts_ref[...] = jnp.broadcast_to(parts[None], parts_ref.shape)


def finish_kernel(parts_ref, residual_ref, image_ref, second_ref, field_ref, left_ref):
    sums = jnp.sum(parts_ref[...], axis=0)
    norm0, first, square, third = (sums[:, at : at + 1] for at in range(4))
    alpha = norm0 / first
    norm1 = norm0 - 2.0 * alpha * first + alpha * alpha * square
    keep = 1.0 + norm1 / norm0
    curv = keep * keep * first - 2.0 * keep * alpha * square + alpha * alpha * third
    beta = norm1 / curv
    residual, image = residual_ref[...], image_ref[...]
    field_ref[...] = (alpha + beta * keep) * residual - (beta * alpha) * image
    left_ref[...] = residual - (alpha + beta * keep) * image + (beta * alpha) * second_ref[...]


def solution(mesh):
    cfg, tm = mesh.shape["cfg"], mesh.shape["tm"]

    def body(targets, features, inv_scales, noise, time_kernel, block_mask):
        rows, width = targets.shape
        count = features.shape[1]
        last = cfg // 2 - 1
        layer, pair = lax.axis_index("tm").reshape(1), (lax.axis_index("cfg") // 2).reshape(1)
        mask = block_mask.reshape(1, rows)

        def shape(*size, kind=F32):
            return jax.ShapeDtypeStruct(size, kind)

        block, row, col = shape(rows, width), pltpu.VMEM((1, rows), F32), shape(rows, 1)
        residual, scaled, flag, ridge = call(
            begin_kernel,
            "begin",
            (pltpu.VMEM((rows, width), F32), pltpu.VMEM((count, rows), F32), row, row),
            targets, features.T, inv_scales.reshape(1, count), mask, noise.reshape(1, rows),
            space=HBM,
            scratch=[
                pltpu.VMEM((rows, width), F32),
                pltpu.VMEM((count, rows), F32),
                pltpu.VMEM((1, count), F32),
                pltpu.VMEM((1, rows), mask.dtype),
                pltpu.SemaphoreType.DMA((5,)),
            ],
            limit=LIMIT,
        )

        half, steps = shape(2 * rows, cfg // 2 * rows, kind=BF16), shape(width, tm * width, kind=BF16)
        groups = [[first + core for first in range(0, cfg, 2)] for core in range(2)]
        every, near = lax.all_gather(scaled, "cfg", axis_index_groups=groups), near_cfg(scaled)
        steps_high, steps_low = call(
            layers_kernel, "layers", (steps, steps), layer, time_kernel, every, near, scalars=1, unread=2
        )
        def over_time(field):
            pieces = gather_tm(field)
            return call(
                steps_kernel, "steps", block, *pieces, steps_high, steps_low
            )

        def over_cfg(pieces, high, low, early):
            partial = call(
                functools.partial(early_kernel, early),
                "early",
                shape(2 * rows, width),
                *[pieces[at] for at in early], high, low,
            )
            own, theirs = call(
                functools.partial(late_kernel, (last,)), "late", (block, block), pieces[last], partial, high, low
            )
            return own, near_cfg(theirs), flag, ridge

        timed = over_time(residual)
        pieces = far_cfg(timed)
        high, low, flag, ridge = call(
            tile_kernel,
            "tile",
            (half, half, col, col),
            pair, near, every, flag, ridge, timed,
            scalars=1,
            unread=1,
        )

        high, pieces[last] = lax.optimization_barrier((high, pieces[last]))
        image = call(image_kernel, "image", block, *over_cfg(pieces, high, low, (0, *range(last - 1, 0, -1))), residual)
        second, sums = call(
            moments_kernel,
            "moments",
            (block, shape(cfg * tm, 1, width)),
            *over_cfg(far_cfg(over_time(image)), high, low, tuple(range(last))), image, residual,
        )
        sums = lax.all_to_all(sums, ("cfg", "tm"), 0, 0, tiled=True)
        return call(finish_kernel, "finish", (block, block), sums, residual, image, second)

    return jax.shard_map(
        body,
        mesh=mesh,
        in_specs=(P("cfg", "tm"), P("cfg", None), P(), P("cfg"), P("tm", None), P("cfg", "tm")),
        out_specs=(P("cfg", "tm"), P("cfg", "tm")),
        check_vma=False,
    )
```

```python
import functools
import math

import jax
import jax.numpy as jnp
from jax import lax
from jax.experimental import pallas as pl
from jax.experimental.pallas import tpu as pltpu
from jax.sharding import PartitionSpec as P

HBM = pl.BlockSpec(memory_space=pltpu.HBM)
ANY = pl.BlockSpec(memory_space=pl.ANY)
VMEM = pl.BlockSpec(memory_space=pltpu.VMEM)
SMEM = pl.BlockSpec(memory_space=pltpu.SMEM)
F32, BF16 = jnp.float32, jnp.bfloat16
LIMIT = 62
LOG2E, LN2 = math.log2(math.e), math.log(2.0)


def partners(axis, offset):
    return [(index, index ^ offset) for index in range(lax.axis_size(axis))]


def far_cfg(block):
    return [block] + [lax.ppermute(block, "cfg", partners("cfg", d)) for d in range(2, lax.axis_size("cfg"), 2)]


def near_cfg(block):
    return lax.ppermute(block, "cfg", partners("cfg", 1))


def offsets_tm(layers):
    return [0] + [d for d in (layers - 1, *range(1, layers - 1)) if d]


def gather_tm(block):
    return [block] + [lax.ppermute(block, "tm", partners("tm", d)) for d in offsets_tm(lax.axis_size("tm"))[1:]]


def call(kernel, name, outs, *args, scalars=0, unread=0, scratch=(), limit=24, space=VMEM, cost=None):
    return pl.pallas_call(
        kernel,
        out_shape=outs,
        in_specs=[SMEM] * scalars + [space] * (len(args) - scalars - unread) + [ANY] * unread,
        cost_estimate=cost,
        out_specs=jax.tree.map(lambda _: VMEM, outs),
        scratch_shapes=list(scratch),
        compiler_params=pltpu.CompilerParams(vmem_limit_bytes=limit * 1024 * 1024),
        name=name,
    )(*args)


def split(value):
    high = value.astype(BF16)
    return high, (value - high.astype(F32)).astype(BF16)


def mul(left, right):
    return jnp.dot(left, right, preferred_element_type=F32)


def mul3(left, right):
    return mul(left[0], right[0]) + (mul(left[0], right[1]) + mul(left[1], right[0]))


def column(row):
    size = min(128, row.shape[1])
    same = lax.broadcasted_iota(jnp.int32, (size, size), 0) == lax.broadcasted_iota(jnp.int32, (size, size), 1)
    return jnp.concatenate(
        [
            jnp.sum(jnp.where(same, row[:, at : at + size], 0.0), axis=1, keepdims=True)
            for at in range(0, row.shape[1], size)
        ],
        axis=0,
    )


def total_of(left, right):
    return jnp.sum(jnp.sum(left * right, axis=0, keepdims=True), axis=1, keepdims=True)


def fetch(pairs, sems):
    copies = [pltpu.make_async_copy(src, dst, sems.at[at]) for at, (src, dst) in enumerate(pairs)]
    for copy in copies:
        copy.start()
    for copy in copies:
        copy.wait()


def begin_kernel(targets_hbm, features_hbm, scales_hbm, mask_hbm, noise_hbm, residual_ref, scaled_ref, *rest):
    flag_ref, ridge_ref, targets_ref, features_ref, scales_ref, mask_ref, sems = rest
    fetch(
        [
            (mask_hbm, mask_ref),
            (targets_hbm, targets_ref),
            (scales_hbm, scales_ref),
            (features_hbm, features_ref),
            (noise_hbm, ridge_ref),
        ],
        sems,
    )
    flag_ref[...] = mask_ref[...].astype(F32)
    residual_ref[...] = column(flag_ref[...]) * targets_ref[...]
    scaled_ref[...] = column(scales_ref[...] * (math.sqrt(3.0) * LOG2E)) * features_ref[...]


def split3(value):
    high, rest = value.astype(BF16), value
    rest = rest - high.astype(F32)
    middle = rest.astype(BF16)
    return high, middle, (rest - middle.astype(F32)).astype(BF16)


def mul_tile(high, low, field):
    width = field.shape[1]
    field_high, field_low = split(field)
    both = mul(high, jnp.concatenate([field_high, field_low], axis=1))
    return both[:, :width] + (both[:, width:] + mul(low, field_high))


def layers_kernel(layer_ref, steps_ref, _, __, high_ref, low_ref):
    width = steps_ref.shape[0]
    for place, offset in enumerate(offsets_tm(steps_ref.shape[1] // width)):
        at = pl.ds(place * width, width)
        high_ref[:, at], low_ref[:, at] = split(
            steps_ref[:, pl.ds(pl.multiple_of((layer_ref[0] ^ offset) * width, width), width)]
        )


def tile_kernel(pair_ref, near_ref, every_ref, mask_ref, noise_ref, _, high_ref, low_ref, flag_ref, ridge_ref):
    flag_ref[...] = column(mask_ref[...])
    ridge_ref[...] = column(noise_ref[...])
    rows, pair = every_ref.shape[2], pair_ref[0]
    pieces = [every_ref.at[pair ^ offset] for offset in range(every_ref.shape[0])]
    left = jnp.transpose(jnp.concatenate([pieces[0][...], near_ref[...]], axis=1))
    left_sq = jnp.sum(left * left, axis=1, keepdims=True)
    high, middle, low = split3(-2.0 * left)
    left = jnp.concatenate([high, high, middle, middle, high, low], axis=1)
    for at, piece in enumerate(pieces):
        right = piece[...]
        right_sq = jnp.sum(right * right, axis=0, keepdims=True)
        high, middle, low = split3(right)
        cross = mul(left, jnp.concatenate([high, middle, high, middle, low, high], axis=0))
        dist2 = jnp.maximum(left_sq + right_sq + cross, 1e-30)
        dist = dist2 * lax.rsqrt(dist2)
        high, low = split((1.0 + LN2 * dist) * jnp.exp2(-dist))
        high_ref[:, pl.ds(at * rows, rows)] = high
        low_ref[:, pl.ds(at * rows, rows)] = low


def mul_t(left, right):
    return lax.dot_general(left, right, (((1,), (1,)), ((), ())), preferred_element_type=F32)


def steps_kernel(*refs):
    pieces, (high_ref, low_ref, out_ref) = refs[:-3], refs[-3:]
    field = split(jnp.concatenate([piece[...] for piece in pieces], axis=1))
    out_ref[...] = mul_t(field[0], high_ref[...]) + (mul_t(field[0], low_ref[...]) + mul_t(field[1], high_ref[...]))


def share(at, pieces, high_ref, low_ref):
    rows = pieces[0].shape[0]
    high, low = (jnp.concatenate([ref[:, pl.ds(place * rows, rows)] for place in at], axis=1) for ref in (high_ref, low_ref))
    return mul_tile(high, low, jnp.concatenate([piece[...] for piece in pieces], axis=0))


def early_kernel(at, *refs):
    pieces, (high_ref, low_ref, out_ref) = refs[:-3], refs[-3:]
    out_ref[...] = share(at, pieces, high_ref, low_ref)


def late_kernel(at, *refs):
    pieces, (early_ref, high_ref, low_ref, own_ref, near_ref) = refs[:-5], refs[-5:]
    mixed = early_ref[...] + share(at, pieces, high_ref, low_ref)
    own_ref[...] = mixed[: own_ref.shape[0]]
    near_ref[...] = mixed[own_ref.shape[0] :]


def rows_share(at, size, pieces, high_ref, low_ref):
    step = high_ref.shape[1] // len(pieces)
    high, low = (
        jnp.concatenate([ref[:, pl.ds(place * step + at, size)] for place in range(len(pieces))], axis=1)
        for ref in (high_ref, low_ref)
    )
    return mul_tile(high, low, jnp.concatenate([piece[...] for piece in pieces], axis=0))


def early_rows_kernel(*refs):
    pieces, (high_ref, low_ref, out_ref) = refs[:-3], refs[-3:]
    out_ref[...] = rows_share(0, pieces[0].shape[0], pieces, high_ref, low_ref)


def late_rows_kernel(*refs):
    pieces, (early_ref, high_ref, low_ref, own_ref, near_ref) = refs[:-5], refs[-5:]
    size = pieces[0].shape[0]
    mixed = early_ref[...] + rows_share(own_ref.shape[0] - size, size, pieces, high_ref, low_ref)
    own_ref[...] = mixed[: own_ref.shape[0]]
    near_ref[...] = mixed[own_ref.shape[0] :]


def image_of(own_ref, near_ref, flag_ref, ridge_ref, field_ref):
    return flag_ref[...] * (own_ref[...] + near_ref[...]) + ridge_ref[...] * field_ref[...]


def image_kernel(*refs):
    image, size = image_of(*refs[:-3]), refs[-2].shape[0]
    refs[-3][...] = image
    refs[-2][...], refs[-1][...] = image[:size], image[size:]


def moments_kernel(*refs):
    image_ref, residual_ref, second_ref, parts_ref = refs[-4:]
    second = image_of(*refs[:-3])
    image, residual = image_ref[...], residual_ref[...]
    second_ref[...] = second
    lane = lax.broadcasted_iota(jnp.int32, parts_ref.shape[1:], 1)
    parts = jnp.zeros(parts_ref.shape[1:], F32)
    for at, pair in enumerate([(residual, residual), (residual, image), (image, image), (image, second)]):
        parts = jnp.where(lane == at, total_of(*pair), parts)
    parts_ref[...] = jnp.broadcast_to(parts[None], parts_ref.shape)


def finish_kernel(parts_ref, residual_ref, image_ref, second_ref, field_ref, left_ref):
    sums = jnp.sum(parts_ref[...], axis=0)
    norm0, first, square, third = (sums[:, at : at + 1] for at in range(4))
    alpha = norm0 / first
    norm1 = norm0 - 2.0 * alpha * first + alpha * alpha * square
    keep = 1.0 + norm1 / norm0
    curv = keep * keep * first - 2.0 * keep * alpha * square + alpha * alpha * third
    beta = norm1 / curv
    residual, image = residual_ref[...], image_ref[...]
    field_ref[...] = (alpha + beta * keep) * residual - (beta * alpha) * image
    left_ref[...] = residual - (alpha + beta * keep) * image + (beta * alpha) * second_ref[...]


def solution(mesh):
    cfg, tm = mesh.shape["cfg"], mesh.shape["tm"]

    def body(targets, features, inv_scales, noise, time_kernel, block_mask):
        rows, width = targets.shape
        count = features.shape[1]
        last = cfg // 2 - 1
        layer, pair = lax.axis_index("tm").reshape(1), (lax.axis_index("cfg") // 2).reshape(1)
        mask = block_mask.reshape(1, rows)

        def shape(*size, kind=F32):
            return jax.ShapeDtypeStruct(size, kind)

        block, row, col = shape(rows, width), pltpu.VMEM((1, rows), F32), shape(rows, 1)
        residual, scaled, flag, ridge = call(
            begin_kernel,
            "begin",
            (pltpu.VMEM((rows, width), F32), pltpu.VMEM((count, rows), F32), row, row),
            targets, features.T, inv_scales.reshape(1, count), mask, noise.reshape(1, rows),
            space=HBM,
            scratch=[
                pltpu.VMEM((rows, width), F32),
                pltpu.VMEM((count, rows), F32),
                pltpu.VMEM((1, count), F32),
                pltpu.VMEM((1, rows), mask.dtype),
                pltpu.SemaphoreType.DMA((5,)),
            ],
            limit=LIMIT,
        )

        half, steps = shape(2 * rows, cfg // 2 * rows, kind=BF16), shape(width, tm * width, kind=BF16)
        groups = [[first + core for first in range(0, cfg, 2)] for core in range(2)]
        every, near = lax.all_gather(scaled, "cfg", axis_index_groups=groups), near_cfg(scaled)
        steps_high, steps_low = call(
            layers_kernel, "layers", (steps, steps), layer, time_kernel, every, near, scalars=1, unread=2
        )
        def over_time(field):
            pieces = gather_tm(field)
            return call(steps_kernel, "steps", shape(*field.shape), *pieces, steps_high, steps_low)

        def over_cfg(pieces, high, low, early):
            partial = call(
                functools.partial(early_kernel, early),
                "early",
                shape(2 * rows, width),
                *[pieces[at] for at in early], high, low,
            )
            own, theirs = call(
                functools.partial(late_kernel, (last,)), "late", (block, block), pieces[last], partial, high, low
            )
            return own, near_cfg(theirs), flag, ridge

        timed = over_time(residual)
        pieces = far_cfg(timed)
        high, low, flag, ridge = call(
            tile_kernel,
            "tile",
            (half, half, col, col),
            pair, near, every, flag, ridge, timed,
            scalars=1,
            unread=1,
        )

        high, pieces[last] = lax.optimization_barrier((high, pieces[last]))
        first = rows * 1 // 2
        image, one, two = call(
            image_kernel,
            "image",
            (block, shape(first, width), shape(rows - first, width)),
            *over_cfg(pieces, high, low, (0, *range(last - 1, 0, -1))), residual,
        )

        ones, twos = far_cfg(over_time(one)), far_cfg(over_time(two))
        partial = call(early_rows_kernel, "early_rows", shape(2 * rows, width), *ones, high, low)
        own, theirs = call(late_rows_kernel, "late_rows", (block, block), *twos, partial, high, low)
        second, sums = call(
            moments_kernel,
            "moments",
            (block, shape(cfg * tm, 1, width)),
            own, near_cfg(theirs), flag, ridge, image, residual,
        )
        sums = lax.all_to_all(sums, ("cfg", "tm"), 0, 0, tiled=True)
        return call(finish_kernel, "finish", (block, block), sums, residual, image, second)

    return jax.shard_map(
        body,
        mesh=mesh,
        in_specs=(P("cfg", "tm"), P("cfg", None), P(), P("cfg"), P("tm", None), P("cfg", "tm")),
        out_specs=(P("cfg", "tm"), P("cfg", "tm")),
        check_vma=False,
    )
```

```python
import functools
import math

import jax
import jax.numpy as jnp
from jax import lax
from jax.experimental import pallas as pl
from jax.experimental.pallas import tpu as pltpu
from jax.sharding import PartitionSpec as P

HBM = pl.BlockSpec(memory_space=pltpu.HBM)
ANY = pl.BlockSpec(memory_space=pl.ANY)
VMEM = pl.BlockSpec(memory_space=pltpu.VMEM)
SMEM = pl.BlockSpec(memory_space=pltpu.SMEM)
F32, BF16 = jnp.float32, jnp.bfloat16
LIMIT = 62
LOG2E, LN2 = math.log2(math.e), math.log(2.0)


def partners(axis, offset):
    return [(index, index ^ offset) for index in range(lax.axis_size(axis))]


def far_cfg(block):
    return [block] + [lax.ppermute(block, "cfg", partners("cfg", d)) for d in range(2, lax.axis_size("cfg"), 2)]


def near_cfg(block):
    return lax.ppermute(block, "cfg", partners("cfg", 1))


def offsets_tm(layers):
    return [0] + [d for d in (layers - 1, *range(1, layers - 1)) if d]


def gather_tm(block):
    return [block] + [lax.ppermute(block, "tm", partners("tm", d)) for d in offsets_tm(lax.axis_size("tm"))[1:]]


def call(kernel, name, outs, *args, scalars=0, unread=0, scratch=(), limit=24, space=VMEM, cost=None):
    return pl.pallas_call(
        kernel,
        out_shape=outs,
        in_specs=[SMEM] * scalars + [space] * (len(args) - scalars - unread) + [ANY] * unread,
        cost_estimate=cost,
        out_specs=jax.tree.map(lambda _: VMEM, outs),
        scratch_shapes=list(scratch),
        compiler_params=pltpu.CompilerParams(vmem_limit_bytes=limit * 1024 * 1024),
        name=name,
    )(*args)


def split(value):
    high = value.astype(BF16)
    return high, (value - high.astype(F32)).astype(BF16)


def mul(left, right):
    return jnp.dot(left, right, preferred_element_type=F32)


def mul3(left, right):
    return mul(left[0], right[0]) + (mul(left[0], right[1]) + mul(left[1], right[0]))


def column(row):
    size = min(128, row.shape[1])
    same = lax.broadcasted_iota(jnp.int32, (size, size), 0) == lax.broadcasted_iota(jnp.int32, (size, size), 1)
    return jnp.concatenate(
        [
            jnp.sum(jnp.where(same, row[:, at : at + size], 0.0), axis=1, keepdims=True)
            for at in range(0, row.shape[1], size)
        ],
        axis=0,
    )


def total_of(left, right):
    return jnp.sum(jnp.sum(left * right, axis=0, keepdims=True), axis=1, keepdims=True)


def fetch(pairs, sems):
    copies = [pltpu.make_async_copy(src, dst, sems.at[at]) for at, (src, dst) in enumerate(pairs)]
    for copy in copies:
        copy.start()
    for copy in copies:
        copy.wait()


def begin_kernel(targets_hbm, features_hbm, scales_hbm, mask_hbm, noise_hbm, residual_ref, scaled_ref, *rest):
    flag_ref, ridge_ref, targets_ref, features_ref, scales_ref, mask_ref, sems = rest
    fetch(
        [
            (mask_hbm, mask_ref),
            (targets_hbm, targets_ref),
            (scales_hbm, scales_ref),
            (features_hbm, features_ref),
            (noise_hbm, ridge_ref),
        ],
        sems,
    )
    flag_ref[...] = mask_ref[...].astype(F32)
    residual_ref[...] = column(flag_ref[...]) * targets_ref[...]
    scaled_ref[...] = column(scales_ref[...] * (math.sqrt(3.0) * LOG2E)) * features_ref[...]


def split3(value):
    high, rest = value.astype(BF16), value
    rest = rest - high.astype(F32)
    middle = rest.astype(BF16)
    return high, middle, (rest - middle.astype(F32)).astype(BF16)


def mul_tile(high, low, field):
    width = field.shape[1]
    field_high, field_low = split(field)
    both = mul(high, jnp.concatenate([field_high, field_low], axis=1))
    return both[:, :width] + (both[:, width:] + mul(low, field_high))


def layers_kernel(layer_ref, steps_ref, _, __, high_ref, low_ref):
    width = steps_ref.shape[0]
    for place, offset in enumerate(offsets_tm(steps_ref.shape[1] // width)):
        at = pl.ds(place * width, width)
        high_ref[:, at], low_ref[:, at] = split(
            steps_ref[:, pl.ds(pl.multiple_of((layer_ref[0] ^ offset) * width, width), width)]
        )


def tile_kernel(pair_ref, near_ref, every_ref, mask_ref, noise_ref, _, high_ref, low_ref, flag_ref, ridge_ref):
    flag_ref[...] = column(mask_ref[...])
    ridge_ref[...] = column(noise_ref[...])
    rows, pair = every_ref.shape[2], pair_ref[0]
    pieces = [every_ref.at[pair ^ offset] for offset in range(every_ref.shape[0])]
    left = jnp.transpose(jnp.concatenate([pieces[0][...], near_ref[...]], axis=1))
    left_sq = jnp.sum(left * left, axis=1, keepdims=True)
    high, middle, low = split3(-2.0 * left)
    left = jnp.concatenate([high, high, middle, middle, high, low], axis=1)
    for at, piece in enumerate(pieces):
        right = piece[...]
        right_sq = jnp.sum(right * right, axis=0, keepdims=True)
        high, middle, low = split3(right)
        cross = mul(left, jnp.concatenate([high, middle, high, middle, low, high], axis=0))
        dist2 = jnp.maximum(left_sq + right_sq + cross, 1e-30)
        dist = dist2 * lax.rsqrt(dist2)
        high, low = split((1.0 + LN2 * dist) * jnp.exp2(-dist))
        high_ref[:, pl.ds(at * rows, rows)] = high
        low_ref[:, pl.ds(at * rows, rows)] = low


def mul_t(left, right):
    return lax.dot_general(left, right, (((1,), (1,)), ((), ())), preferred_element_type=F32)


def steps_kernel(places, *refs):
    pieces, (high_ref, low_ref, out_ref) = refs[:-3], refs[-3:]
    pieces = [pieces[places.index(at)] for at in range(len(pieces))]
    field = split(jnp.concatenate([piece[...] for piece in pieces], axis=1))
    out_ref[...] = mul_t(field[0], high_ref[...]) + (mul_t(field[0], low_ref[...]) + mul_t(field[1], high_ref[...]))


def share(at, pieces, high_ref, low_ref):
    rows = pieces[0].shape[0]
    high, low = (jnp.concatenate([ref[:, pl.ds(place * rows, rows)] for place in at], axis=1) for ref in (high_ref, low_ref))
    return mul_tile(high, low, jnp.concatenate([piece[...] for piece in pieces], axis=0))


def early_kernel(at, *refs):
    pieces, (high_ref, low_ref, out_ref) = refs[:-3], refs[-3:]
    out_ref[...] = share(at, pieces, high_ref, low_ref)


def late_kernel(at, *refs):
    pieces, (early_ref, high_ref, low_ref, own_ref, near_ref) = refs[:-5], refs[-5:]
    mixed = early_ref[...] + share(at, pieces, high_ref, low_ref)
    own_ref[...] = mixed[: own_ref.shape[0]]
    near_ref[...] = mixed[own_ref.shape[0] :]


def rows_share(at, size, pieces, high_ref, low_ref):
    step = high_ref.shape[1] // len(pieces)
    high, low = (
        jnp.concatenate([ref[:, pl.ds(place * step + at, size)] for place in range(len(pieces))], axis=1)
        for ref in (high_ref, low_ref)
    )
    return mul_tile(high, low, jnp.concatenate([piece[...] for piece in pieces], axis=0))


def early_rows_kernel(*refs):
    pieces, (high_ref, low_ref, out_ref) = refs[:-3], refs[-3:]
    out_ref[...] = rows_share(0, pieces[0].shape[0], pieces, high_ref, low_ref)


def late_rows_kernel(*refs):
    pieces, (early_ref, high_ref, low_ref, ridge_ref, image_ref, image_near_ref, residual_ref) = refs[:-10], refs[-10:-3]
    own_ref, near_ref, parts_ref = refs[-3:]
    size = pieces[0].shape[0]
    mixed = early_ref[...] + rows_share(own_ref.shape[0] - size, size, pieces, high_ref, low_ref)
    own, near = mixed[: own_ref.shape[0]], mixed[own_ref.shape[0] :]
    own_ref[...], near_ref[...] = own, near
    image, residual = image_ref[...], residual_ref[...]
    third = total_of(image, own + ridge_ref[...] * image) + total_of(image_near_ref[...], near)
    lane = lax.broadcasted_iota(jnp.int32, parts_ref.shape[1:], 1)
    parts = jnp.where(lane == 3, third, jnp.zeros(parts_ref.shape[1:], F32))
    for at, pair in enumerate([(residual, residual), (residual, image), (image, image)]):
        parts = jnp.where(lane == at, total_of(*pair), parts)
    parts_ref[...] = jnp.broadcast_to(parts[None], parts_ref.shape)


def image_of(own_ref, near_ref, flag_ref, ridge_ref, field_ref):
    return flag_ref[...] * (own_ref[...] + near_ref[...]) + ridge_ref[...] * field_ref[...]


def image_kernel(*refs):
    image, size = image_of(*refs[:-3]), refs[-2].shape[0]
    refs[-3][...] = image
    refs[-2][...], refs[-1][...] = image[:size], image[size:]


def finish_kernel(parts_ref, residual_ref, own_ref, near_ref, flag_ref, ridge_ref, image_ref, field_ref, left_ref):
    sums = jnp.sum(parts_ref[...], axis=0)
    norm0, first, square, third = (sums[:, at : at + 1] for at in range(4))
    alpha = norm0 / first
    norm1 = norm0 - 2.0 * alpha * first + alpha * alpha * square
    keep = 1.0 + norm1 / norm0
    curv = keep * keep * first - 2.0 * keep * alpha * square + alpha * alpha * third
    beta = norm1 / curv
    residual, image = residual_ref[...], image_ref[...]
    second = image_of(own_ref, near_ref, flag_ref, ridge_ref, image_ref)
    field_ref[...] = (alpha + beta * keep) * residual - (beta * alpha) * image
    left_ref[...] = residual - (alpha + beta * keep) * image + (beta * alpha) * second


def solution(mesh):
    cfg, tm = mesh.shape["cfg"], mesh.shape["tm"]

    def body(targets, features, inv_scales, noise, time_kernel, block_mask):
        rows, width = targets.shape
        count = features.shape[1]
        last = cfg // 2 - 1
        layer, pair = lax.axis_index("tm").reshape(1), (lax.axis_index("cfg") // 2).reshape(1)
        mask = block_mask.reshape(1, rows)

        def shape(*size, kind=F32):
            return jax.ShapeDtypeStruct(size, kind)

        block, row, col = shape(rows, width), pltpu.VMEM((1, rows), F32), shape(rows, 1)
        residual, scaled, flag, ridge = call(
            begin_kernel,
            "begin",
            (pltpu.VMEM((rows, width), F32), pltpu.VMEM((count, rows), F32), row, row),
            targets, features.T, inv_scales.reshape(1, count), mask, noise.reshape(1, rows),
            space=HBM,
            scratch=[
                pltpu.VMEM((rows, width), F32),
                pltpu.VMEM((count, rows), F32),
                pltpu.VMEM((1, count), F32),
                pltpu.VMEM((1, rows), mask.dtype),
                pltpu.SemaphoreType.DMA((5,)),
            ],
            limit=LIMIT,
        )

        half, steps = shape(2 * rows, cfg // 2 * rows, kind=BF16), shape(width, tm * width, kind=BF16)
        groups = [[first + core for first in range(0, cfg, 2)] for core in range(2)]
        every, near = lax.all_gather(scaled, "cfg", axis_index_groups=groups), near_cfg(scaled)
        steps_high, steps_low = call(
            layers_kernel, "layers", (steps, steps), layer, time_kernel, every, near, scalars=1, unread=2
        )
        def over_time(field, *places):
            pieces, places = gather_tm(field), places or tuple(range(tm))
            return call(
                functools.partial(steps_kernel, places),
                "steps",
                shape(*field.shape),
                *[pieces[at] for at in places], steps_high, steps_low,
            )

        def over_cfg(pieces, high, low, early):
            partial = call(
                functools.partial(early_kernel, early),
                "early",
                shape(2 * rows, width),
                *[pieces[at] for at in early], high, low,
            )
            own, theirs = call(
                functools.partial(late_kernel, (last,)), "late", (block, block), pieces[last], partial, high, low
            )
            return own, near_cfg(theirs), flag, ridge

        timed = over_time(residual)
        pieces = far_cfg(timed)
        high, low, flag, ridge = call(
            tile_kernel,
            "tile",
            (half, half, col, col),
            pair, near, every, flag, ridge, timed,
            scalars=1,
            unread=1,
        )

        high, pieces[last] = lax.optimization_barrier((high, pieces[last]))
        first = rows * 1 // 2
        image, one, two = call(
            image_kernel,
            "image",
            (block, shape(first, width), shape(rows - first, width)),
            *over_cfg(pieces, high, low, (0, *range(last - 1, 0, -1))), residual,
        )

        ones, twos = far_cfg(over_time(one)), far_cfg(over_time(two, 0, *range(2, tm), 1))
        partial = call(early_rows_kernel, "early_rows", shape(2 * rows, width), *ones, high, low)
        own, theirs, sums = call(
            late_rows_kernel,
            "late_rows",
            (block, block, shape(cfg * tm, 1, width)),
            *twos, partial, high, low, ridge, image, near_cfg(image), residual,
        )
        sums = lax.all_to_all(sums, ("cfg", "tm"), 0, 0, tiled=True)
        return call(
            finish_kernel, "finish", (block, block), sums, residual, own, near_cfg(theirs), flag, ridge, image
        )

    return jax.shard_map(
        body,
        mesh=mesh,
        in_specs=(P("cfg", "tm"), P("cfg", None), P(), P("cfg"), P("tm", None), P("cfg", "tm")),
        out_specs=(P("cfg", "tm"), P("cfg", "tm")),
        check_vma=False,
    )
```

```python
import functools
import math

import jax
import jax.numpy as jnp
from jax import lax
from jax.experimental import pallas as pl
from jax.experimental.pallas import tpu as pltpu
from jax.sharding import PartitionSpec as P

HBM = pl.BlockSpec(memory_space=pltpu.HBM)
ANY = pl.BlockSpec(memory_space=pl.ANY)
VMEM = pl.BlockSpec(memory_space=pltpu.VMEM)
SMEM = pl.BlockSpec(memory_space=pltpu.SMEM)
F32, BF16 = jnp.float32, jnp.bfloat16
LIMIT = 62
LOG2E, LN2 = math.log2(math.e), math.log(2.0)


def partners(axis, offset):
    return [(index, index ^ offset) for index in range(lax.axis_size(axis))]


def far_cfg(block):
    return [block] + [lax.ppermute(block, "cfg", partners("cfg", d)) for d in range(2, lax.axis_size("cfg"), 2)]


def near_cfg(block):
    return lax.ppermute(block, "cfg", partners("cfg", 1))


def offsets_tm(layers):
    return [0] + [d for d in (layers - 1, *range(1, layers - 1)) if d]


def gather_tm(block):
    return [block] + [lax.ppermute(block, "tm", partners("tm", d)) for d in offsets_tm(lax.axis_size("tm"))[1:]]


def call(kernel, name, outs, *args, scalars=0, unread=0, scratch=(), limit=24, space=VMEM, cost=None):
    return pl.pallas_call(
        kernel,
        out_shape=outs,
        in_specs=[SMEM] * scalars + [space] * (len(args) - scalars - unread) + [ANY] * unread,
        cost_estimate=cost,
        out_specs=jax.tree.map(lambda _: VMEM, outs),
        scratch_shapes=list(scratch),
        compiler_params=pltpu.CompilerParams(vmem_limit_bytes=limit * 1024 * 1024),
        name=name,
    )(*args)


def split(value):
    high = value.astype(BF16)
    return high, (value - high.astype(F32)).astype(BF16)


def mul(left, right):
    return jnp.dot(left, right, preferred_element_type=F32)


def mul3(left, right):
    return mul(left[0], right[0]) + (mul(left[0], right[1]) + mul(left[1], right[0]))


def column(row):
    size = min(128, row.shape[1])
    same = lax.broadcasted_iota(jnp.int32, (size, size), 0) == lax.broadcasted_iota(jnp.int32, (size, size), 1)
    return jnp.concatenate(
        [
            jnp.sum(jnp.where(same, row[:, at : at + size], 0.0), axis=1, keepdims=True)
            for at in range(0, row.shape[1], size)
        ],
        axis=0,
    )


def total_of(left, right):
    return jnp.sum(jnp.sum(left * right, axis=0, keepdims=True), axis=1, keepdims=True)


def fetch(pairs, sems):
    copies = [pltpu.make_async_copy(src, dst, sems.at[at]) for at, (src, dst) in enumerate(pairs)]
    for copy in copies:
        copy.start()
    for copy in copies:
        copy.wait()


def begin_kernel(targets_hbm, features_hbm, scales_hbm, mask_hbm, noise_hbm, residual_ref, scaled_ref, *rest):
    flag_ref, ridge_ref, targets_ref, features_ref, scales_ref, mask_ref, sems = rest
    fetch(
        [
            (mask_hbm, mask_ref),
            (targets_hbm, targets_ref),
            (scales_hbm, scales_ref),
            (features_hbm, features_ref),
            (noise_hbm, ridge_ref),
        ],
        sems,
    )
    flag_ref[...] = mask_ref[...].astype(F32)
    residual_ref[...] = column(flag_ref[...]) * targets_ref[...]
    scaled_ref[...] = column(scales_ref[...] * (math.sqrt(3.0) * LOG2E)) * features_ref[...]


def split3(value):
    high, rest = value.astype(BF16), value
    rest = rest - high.astype(F32)
    middle = rest.astype(BF16)
    return high, middle, (rest - middle.astype(F32)).astype(BF16)


def mul_tile(high, low, field):
    width = field.shape[1]
    field_high, field_low = split(field)
    both = mul(high, jnp.concatenate([field_high, field_low], axis=1))
    return both[:, :width] + (both[:, width:] + mul(low, field_high))


def layers_kernel(layer_ref, steps_ref, _, __, high_ref, low_ref):
    width = steps_ref.shape[0]
    for place, offset in enumerate(offsets_tm(steps_ref.shape[1] // width)):
        at = pl.ds(place * width, width)
        high_ref[:, at], low_ref[:, at] = split(
            steps_ref[:, pl.ds(pl.multiple_of((layer_ref[0] ^ offset) * width, width), width)]
        )


def tile_kernel(pair_ref, near_ref, every_ref, mask_ref, noise_ref, _, high_ref, low_ref, flag_ref, ridge_ref):
    flag_ref[...] = column(mask_ref[...])
    ridge_ref[...] = column(noise_ref[...])
    rows, pair = every_ref.shape[2], pair_ref[0]
    pieces = [every_ref.at[pair ^ offset] for offset in range(every_ref.shape[0])]
    left = jnp.transpose(jnp.concatenate([pieces[0][...], near_ref[...]], axis=1))
    left_sq = jnp.sum(left * left, axis=1, keepdims=True)
    high, middle, low = split3(-2.0 * left)
    left = jnp.concatenate([high, high, middle, middle, high, low], axis=1)
    for at, piece in enumerate(pieces):
        right = piece[...]
        right_sq = jnp.sum(right * right, axis=0, keepdims=True)
        high, middle, low = split3(right)
        cross = mul(left, jnp.concatenate([high, middle, high, middle, low, high], axis=0))
        dist2 = jnp.maximum(left_sq + right_sq + cross, 1e-30)
        dist = dist2 * lax.rsqrt(dist2)
        high, low = split((1.0 + LN2 * dist) * jnp.exp2(-dist))
        high_ref[:, pl.ds(at * rows, rows)] = high
        low_ref[:, pl.ds(at * rows, rows)] = low


def mul_t(left, right):
    return lax.dot_general(left, right, (((1,), (1,)), ((), ())), preferred_element_type=F32)


def steps_kernel(places, *refs):
    pieces, (high_ref, low_ref, out_ref) = refs[:-3], refs[-3:]
    pieces = [pieces[places.index(at)] for at in range(len(pieces))]
    field = split(jnp.concatenate([piece[...] for piece in pieces], axis=1))
    out_ref[...] = mul_t(field[0], high_ref[...]) + (mul_t(field[0], low_ref[...]) + mul_t(field[1], high_ref[...]))


def share(at, pieces, high_ref, low_ref):
    rows = pieces[0].shape[0]
    high, low = (jnp.concatenate([ref[:, pl.ds(place * rows, rows)] for place in at], axis=1) for ref in (high_ref, low_ref))
    return mul_tile(high, low, jnp.concatenate([piece[...] for piece in pieces], axis=0))


def early_kernel(at, *refs):
    pieces, (high_ref, low_ref, out_ref) = refs[:-3], refs[-3:]
    out_ref[...] = share(at, pieces, high_ref, low_ref)


def late_kernel(at, *refs):
    pieces, (early_ref, high_ref, low_ref, own_ref, near_ref) = refs[:-5], refs[-5:]
    mixed = early_ref[...] + share(at, pieces, high_ref, low_ref)
    own_ref[...] = mixed[: own_ref.shape[0]]
    near_ref[...] = mixed[own_ref.shape[0] :]


def rows_share(at, size, pieces, high_ref, low_ref):
    step = high_ref.shape[1] // len(pieces)
    high, low = (
        jnp.concatenate([ref[:, pl.ds(place * step + at, size)] for place in range(len(pieces))], axis=1)
        for ref in (high_ref, low_ref)
    )
    return mul_tile(high, low, jnp.concatenate([piece[...] for piece in pieces], axis=0))


def early_rows_kernel(*refs):
    pieces, (high_ref, low_ref, out_ref) = refs[:-3], refs[-3:]
    out_ref[...] = rows_share(0, pieces[0].shape[0], pieces, high_ref, low_ref)


def late_rows_kernel(*refs):
    pieces, (early_ref, high_ref, low_ref, ridge_ref, image_ref, image_near_ref, residual_ref) = refs[:-10], refs[-10:-3]
    own_ref, near_ref, parts_ref = refs[-3:]
    size = pieces[0].shape[0]
    mixed = early_ref[...] + rows_share(own_ref.shape[0] - size, size, pieces, high_ref, low_ref)
    own, near = mixed[: own_ref.shape[0]], mixed[own_ref.shape[0] :]
    own_ref[...], near_ref[...] = own, near
    image, residual = image_ref[...], residual_ref[...]
    third = total_of(image, own + ridge_ref[...] * image) + total_of(image_near_ref[...], near)
    lane = lax.broadcasted_iota(jnp.int32, parts_ref.shape[1:], 1)
    parts = jnp.where(lane == 3, third, jnp.zeros(parts_ref.shape[1:], F32))
    for at, pair in enumerate([(residual, residual), (residual, image), (image, image)]):
        parts = jnp.where(lane == at, total_of(*pair), parts)
    parts_ref[...] = jnp.broadcast_to(parts[None], parts_ref.shape)


def image_of(own_ref, near_ref, flag_ref, ridge_ref, field_ref):
    return flag_ref[...] * (own_ref[...] + near_ref[...]) + ridge_ref[...] * field_ref[...]


def image_kernel(*refs):
    image, size = image_of(*refs[:-3]), refs[-2].shape[0]
    refs[-3][...] = image
    refs[-2][...], refs[-1][...] = image[:size], image[size:]


def finish_kernel(parts_ref, residual_ref, own_ref, near_ref, flag_ref, ridge_ref, image_ref, field_ref, left_ref):
    sums = jnp.sum(parts_ref[...], axis=0)
    norm0, first, square, third = (sums[:, at : at + 1] for at in range(4))
    alpha = norm0 / first
    norm1 = norm0 - 2.0 * alpha * first + alpha * alpha * square
    keep = 1.0 + norm1 / norm0
    curv = keep * keep * first - 2.0 * keep * alpha * square + alpha * alpha * third
    beta = norm1 / curv
    residual, image = residual_ref[...], image_ref[...]
    second = image_of(own_ref, near_ref, flag_ref, ridge_ref, image_ref)
    field_ref[...] = (alpha + beta * keep) * residual - (beta * alpha) * image
    left_ref[...] = residual - (alpha + beta * keep) * image + (beta * alpha) * second


def solution(mesh):
    cfg, tm = mesh.shape["cfg"], mesh.shape["tm"]

    def body(targets, features, inv_scales, noise, time_kernel, block_mask):
        rows, width = targets.shape
        count = features.shape[1]
        last = cfg // 2 - 1
        layer, pair = lax.axis_index("tm").reshape(1), (lax.axis_index("cfg") // 2).reshape(1)
        mask = block_mask.reshape(1, rows)

        def shape(*size, kind=F32):
            return jax.ShapeDtypeStruct(size, kind)

        block, row, col = shape(rows, width), pltpu.VMEM((1, rows), F32), shape(rows, 1)
        residual, scaled, flag, ridge = call(
            begin_kernel,
            "begin",
            (pltpu.VMEM((rows, width), F32), pltpu.VMEM((count, rows), F32), row, row),
            targets, features.T, inv_scales.reshape(1, count), mask, noise.reshape(1, rows),
            space=HBM,
            scratch=[
                pltpu.VMEM((rows, width), F32),
                pltpu.VMEM((count, rows), F32),
                pltpu.VMEM((1, count), F32),
                pltpu.VMEM((1, rows), mask.dtype),
                pltpu.SemaphoreType.DMA((5,)),
            ],
            limit=LIMIT,
        )

        half, steps = shape(2 * rows, cfg // 2 * rows, kind=BF16), shape(width, tm * width, kind=BF16)
        groups = [[first + core for first in range(0, cfg, 2)] for core in range(2)]
        every, near = lax.all_gather(scaled, "cfg", axis_index_groups=groups), near_cfg(scaled)
        steps_high, steps_low = call(
            layers_kernel, "layers", (steps, steps), layer, time_kernel, every, near, scalars=1, unread=2
        )
        def over_time(field, *places):
            pieces, places = gather_tm(field), places or tuple(range(tm))
            return call(
                functools.partial(steps_kernel, places),
                "steps",
                shape(*field.shape),
                *[pieces[at] for at in places], steps_high, steps_low,
            )

        def over_cfg(pieces, high, low, early, late):
            partial = call(
                functools.partial(early_kernel, early),
                "early",
                shape(2 * rows, width),
                *[pieces[at] for at in early], high, low,
            )
            own, theirs = call(
                functools.partial(late_kernel, late),
                "late",
                (block, block),
                *[pieces[at] for at in late], partial, high, low,
            )
            return own, near_cfg(theirs), flag, ridge

        timed = over_time(residual, 0, 1, *range(tm - 1, 1, -1))
        pieces = far_cfg(timed)
        high, low, flag, ridge = call(
            tile_kernel,
            "tile",
            (half, half, col, col),
            pair, near, every, flag, ridge, timed,
            scalars=1,
            unread=1,
        )

        high, pieces[last] = lax.optimization_barrier((high, pieces[last]))
        first = rows * 1 // 2
        image, one, two = call(
            image_kernel,
            "image",
            (block, shape(first, width), shape(rows - first, width)),
            *over_cfg(pieces, high, low, (0, last), tuple(range(last - 1, 0, -1))), residual,
        )

        ones, twos = far_cfg(over_time(one)), far_cfg(over_time(two, 0, *range(2, tm), 1))
        partial = call(early_rows_kernel, "early_rows", shape(2 * rows, width), *ones, high, low)
        own, theirs, sums = call(
            late_rows_kernel,
            "late_rows",
            (block, block, shape(cfg * tm, 1, width)),
            *twos, partial, high, low, ridge, image, near_cfg(image), residual,
        )
        sums = lax.all_to_all(sums, ("cfg", "tm"), 0, 0, tiled=True)
        return call(
            finish_kernel, "finish", (block, block), sums, residual, own, near_cfg(theirs), flag, ridge, image
        )

    return jax.shard_map(
        body,
        mesh=mesh,
        in_specs=(P("cfg", "tm"), P("cfg", None), P(), P("cfg"), P("tm", None), P("cfg", "tm")),
        out_specs=(P("cfg", "tm"), P("cfg", "tm")),
        check_vma=False,
    )
```

```python
import functools
import math

import jax
import jax.numpy as jnp
from jax import lax
from jax.experimental import pallas as pl
from jax.experimental.pallas import tpu as pltpu
from jax.sharding import PartitionSpec as P

HBM = pl.BlockSpec(memory_space=pltpu.HBM)
ANY = pl.BlockSpec(memory_space=pl.ANY)
VMEM = pl.BlockSpec(memory_space=pltpu.VMEM)
SMEM = pl.BlockSpec(memory_space=pltpu.SMEM)
F32, BF16 = jnp.float32, jnp.bfloat16
LIMIT = 62
LOG2E, LN2 = math.log2(math.e), math.log(2.0)


def partners(axis, offset):
    return [(index, index ^ offset) for index in range(lax.axis_size(axis))]


def far_cfg(block):
    return [block] + [lax.ppermute(block, "cfg", partners("cfg", d)) for d in range(2, lax.axis_size("cfg"), 2)]


def near_cfg(block):
    return lax.ppermute(block, "cfg", partners("cfg", 1))


def offsets_tm(layers):
    return [0] + [d for d in (layers - 1, *range(1, layers - 1)) if d]


def gather_tm(block):
    return [block] + [lax.ppermute(block, "tm", partners("tm", d)) for d in offsets_tm(lax.axis_size("tm"))[1:]]


def call(kernel, name, outs, *args, scalars=0, unread=0, scratch=(), limit=24, space=VMEM, cost=None):
    return pl.pallas_call(
        kernel,
        out_shape=outs,
        in_specs=[SMEM] * scalars + [space] * (len(args) - scalars - unread) + [ANY] * unread,
        cost_estimate=cost,
        out_specs=jax.tree.map(lambda _: VMEM, outs),
        scratch_shapes=list(scratch),
        compiler_params=pltpu.CompilerParams(vmem_limit_bytes=limit * 1024 * 1024),
        name=name,
    )(*args)


def split(value):
    high = value.astype(BF16)
    return high, (value - high.astype(F32)).astype(BF16)


def mul(left, right):
    return jnp.dot(left, right, preferred_element_type=F32)


def mul3(left, right):
    return mul(left[0], right[0]) + (mul(left[0], right[1]) + mul(left[1], right[0]))


def column(row):
    size = min(128, row.shape[1])
    same = lax.broadcasted_iota(jnp.int32, (size, size), 0) == lax.broadcasted_iota(jnp.int32, (size, size), 1)
    return jnp.concatenate(
        [
            jnp.sum(jnp.where(same, row[:, at : at + size], 0.0), axis=1, keepdims=True)
            for at in range(0, row.shape[1], size)
        ],
        axis=0,
    )


def total_of(left, right):
    return jnp.sum(jnp.sum(left * right, axis=0, keepdims=True), axis=1, keepdims=True)


def fetch(pairs, sems):
    copies = [pltpu.make_async_copy(src, dst, sems.at[at]) for at, (src, dst) in enumerate(pairs)]
    for copy in copies:
        copy.start()
    for copy in copies:
        copy.wait()


def begin_kernel(targets_hbm, features_hbm, scales_hbm, mask_hbm, noise_hbm, residual_ref, scaled_ref, *rest):
    flag_ref, ridge_ref, targets_ref, features_ref, scales_ref, mask_ref, sems = rest
    fetch(
        [
            (mask_hbm, mask_ref),
            (targets_hbm, targets_ref),
            (scales_hbm, scales_ref),
            (features_hbm, features_ref),
            (noise_hbm, ridge_ref),
        ],
        sems,
    )
    flag_ref[...] = mask_ref[...].astype(F32)
    residual_ref[...] = column(flag_ref[...]) * targets_ref[...]
    scaled_ref[...] = column(scales_ref[...] * (math.sqrt(3.0) * LOG2E)) * features_ref[...]


def split3(value):
    high, rest = value.astype(BF16), value
    rest = rest - high.astype(F32)
    middle = rest.astype(BF16)
    return high, middle, (rest - middle.astype(F32)).astype(BF16)


def mul_tile(high, low, field):
    width = field.shape[1]
    field_high, field_low = split(field)
    both = mul(high, jnp.concatenate([field_high, field_low], axis=1))
    return both[:, :width] + (both[:, width:] + mul(low, field_high))


def layers_kernel(layer_ref, steps_ref, _, high_ref, low_ref):
    width = steps_ref.shape[0]
    for place, offset in enumerate(offsets_tm(steps_ref.shape[1] // width)):
        at = pl.ds(place * width, width)
        high_ref[:, at], low_ref[:, at] = split(
            steps_ref[:, pl.ds(pl.multiple_of((layer_ref[0] ^ offset) * width, width), width)]
        )


def tile_kernel(pair_ref, near_ref, every_ref, mask_ref, noise_ref, _, high_ref, low_ref, flag_ref, ridge_ref):
    flag_ref[...] = column(mask_ref[...])
    ridge_ref[...] = column(noise_ref[...])
    rows, pair = every_ref.shape[2], pair_ref[0]
    pieces = [every_ref.at[pair ^ offset] for offset in range(every_ref.shape[0])]
    left = jnp.transpose(jnp.concatenate([pieces[0][...], near_ref[...]], axis=1))
    left_sq = jnp.sum(left * left, axis=1, keepdims=True)
    high, middle, low = split3(-2.0 * left)
    left = jnp.concatenate([high, high, middle, middle, high, low], axis=1)
    for at, piece in enumerate(pieces):
        right = piece[...]
        right_sq = jnp.sum(right * right, axis=0, keepdims=True)
        high, middle, low = split3(right)
        cross = mul(left, jnp.concatenate([high, middle, high, middle, low, high], axis=0))
        dist2 = jnp.maximum(left_sq + right_sq + cross, 1e-30)
        dist = dist2 * lax.rsqrt(dist2)
        high, low = split((1.0 + LN2 * dist) * jnp.exp2(-dist))
        high_ref[:, pl.ds(at * rows, rows)] = high
        low_ref[:, pl.ds(at * rows, rows)] = low


def mul_t(left, right):
    return lax.dot_general(left, right, (((1,), (1,)), ((), ())), preferred_element_type=F32)


def steps_kernel(places, *refs):
    pieces, (high_ref, low_ref, out_ref) = refs[:-3], refs[-3:]
    pieces = [pieces[places.index(at)] for at in range(len(pieces))]
    field = split(jnp.concatenate([piece[...] for piece in pieces], axis=1))
    out_ref[...] = mul_t(field[0], high_ref[...]) + (mul_t(field[0], low_ref[...]) + mul_t(field[1], high_ref[...]))


def share(at, pieces, high_ref, low_ref):
    rows = pieces[0].shape[0]
    high, low = (jnp.concatenate([ref[:, pl.ds(place * rows, rows)] for place in at], axis=1) for ref in (high_ref, low_ref))
    return mul_tile(high, low, jnp.concatenate([piece[...] for piece in pieces], axis=0))


def early_kernel(at, *refs):
    pieces, (high_ref, low_ref, out_ref) = refs[:-3], refs[-3:]
    out_ref[...] = share(at, pieces, high_ref, low_ref)


def late_kernel(at, *refs):
    pieces, (early_ref, high_ref, low_ref, own_ref, near_ref) = refs[:-5], refs[-5:]
    mixed = early_ref[...] + share(at, pieces, high_ref, low_ref)
    own_ref[...] = mixed[: own_ref.shape[0]]
    near_ref[...] = mixed[own_ref.shape[0] :]


def rows_share(at, size, places, blocks, pieces, high_ref, low_ref):
    step = high_ref.shape[1] // blocks
    high, low = (
        jnp.concatenate([ref[:, pl.ds(place * step + at, size)] for place in places], axis=1)
        for ref in (high_ref, low_ref)
    )
    return mul_tile(high, low, jnp.concatenate([piece[...] for piece in pieces], axis=0))


def early_rows_kernel(*refs):
    pieces, (high_ref, low_ref, out_ref) = refs[:-3], refs[-3:]
    out_ref[...] = rows_share(0, pieces[0].shape[0], range(len(pieces)), len(pieces), pieces, high_ref, low_ref)


def middle_rows_kernel(blocks, *refs):
    pieces, (early_ref, high_ref, low_ref, out_ref) = refs[:-4], refs[-4:]
    size = pieces[0].shape[0]
    share_of = rows_share(out_ref.shape[0] // 2 - size, size, range(len(pieces)), blocks, pieces, high_ref, low_ref)
    out_ref[...] = early_ref[...] + share_of


def late_rows_kernel(blocks, *refs):
    pieces, (early_ref, high_ref, low_ref, ridge_ref, image_ref, image_near_ref, residual_ref) = refs[:-10], refs[-10:-3]
    own_ref, near_ref, parts_ref = refs[-3:]
    size = pieces[0].shape[0]
    mixed = early_ref[...] + rows_share(
        own_ref.shape[0] - size, size, range(blocks - len(pieces), blocks), blocks, pieces, high_ref, low_ref
    )
    own, near = mixed[: own_ref.shape[0]], mixed[own_ref.shape[0] :]
    own_ref[...], near_ref[...] = own, near
    image, residual = image_ref[...], residual_ref[...]
    third = total_of(image, own + ridge_ref[...] * image) + total_of(image_near_ref[...], near)
    lane = lax.broadcasted_iota(jnp.int32, parts_ref.shape[1:], 1)
    parts = jnp.where(lane == 3, third, jnp.zeros(parts_ref.shape[1:], F32))
    for at, pair in enumerate([(residual, residual), (residual, image), (image, image)]):
        parts = jnp.where(lane == at, total_of(*pair), parts)
    parts_ref[...] = jnp.broadcast_to(parts[None], parts_ref.shape)


def image_of(own_ref, near_ref, flag_ref, ridge_ref, field_ref):
    return flag_ref[...] * (own_ref[...] + near_ref[...]) + ridge_ref[...] * field_ref[...]


def image_kernel(*refs):
    image, size = image_of(*refs[:-3]), refs[-2].shape[0]
    refs[-3][...] = image
    refs[-2][...], refs[-1][...] = image[:size], image[size:]


def finish_kernel(parts_ref, residual_ref, own_ref, near_ref, flag_ref, ridge_ref, image_ref, field_ref, left_ref):
    sums = jnp.sum(parts_ref[...], axis=0)
    norm0, first, square, third = (sums[:, at : at + 1] for at in range(4))
    alpha = norm0 / first
    norm1 = norm0 - 2.0 * alpha * first + alpha * alpha * square
    keep = 1.0 + norm1 / norm0
    curv = keep * keep * first - 2.0 * keep * alpha * square + alpha * alpha * third
    beta = norm1 / curv
    residual, image = residual_ref[...], image_ref[...]
    second = image_of(own_ref, near_ref, flag_ref, ridge_ref, image_ref)
    field_ref[...] = (alpha + beta * keep) * residual - (beta * alpha) * image
    left_ref[...] = residual - (alpha + beta * keep) * image + (beta * alpha) * second


def solution(mesh):
    cfg, tm = mesh.shape["cfg"], mesh.shape["tm"]

    def body(targets, features, inv_scales, noise, time_kernel, block_mask):
        rows, width = targets.shape
        count = features.shape[1]
        last = cfg // 2 - 1
        layer, pair = lax.axis_index("tm").reshape(1), (lax.axis_index("cfg") // 2).reshape(1)
        mask = block_mask.reshape(1, rows)

        def shape(*size, kind=F32):
            return jax.ShapeDtypeStruct(size, kind)

        block, row, col = shape(rows, width), pltpu.VMEM((1, rows), F32), shape(rows, 1)
        residual, scaled, flag, ridge = call(
            begin_kernel,
            "begin",
            (pltpu.VMEM((rows, width), F32), pltpu.VMEM((count, rows), F32), row, row),
            targets, features.T, inv_scales.reshape(1, count), mask, noise.reshape(1, rows),
            space=HBM,
            scratch=[
                pltpu.VMEM((rows, width), F32),
                pltpu.VMEM((count, rows), F32),
                pltpu.VMEM((1, count), F32),
                pltpu.VMEM((1, rows), mask.dtype),
                pltpu.SemaphoreType.DMA((5,)),
            ],
            limit=LIMIT,
        )

        half, steps = shape(2 * rows, cfg // 2 * rows, kind=BF16), shape(width, tm * width, kind=BF16)
        groups = [[first + core for first in range(0, cfg, 2)] for core in range(2)]
        every, near = lax.all_gather(scaled, "cfg", axis_index_groups=groups), near_cfg(scaled)
        steps_high, steps_low = call(
            layers_kernel, "layers", (steps, steps), layer, time_kernel, every, scalars=1, unread=1
        )
        def over_time(field, *places):
            pieces, places = gather_tm(field), places or tuple(range(tm))
            return call(
                functools.partial(steps_kernel, places),
                "steps",
                shape(*field.shape),
                *[pieces[at] for at in places], steps_high, steps_low,
            )

        def over_cfg(pieces, high, low, early, late):
            partial = call(
                functools.partial(early_kernel, early),
                "early",
                shape(2 * rows, width),
                *[pieces[at] for at in early], high, low,
            )
            own, theirs = call(
                functools.partial(late_kernel, late),
                "late",
                (block, block),
                *[pieces[at] for at in late], partial, high, low,
            )
            return own, near_cfg(theirs), flag, ridge

        timed = over_time(residual, 0, 1, *range(tm - 1, 1, -1))
        pieces = far_cfg(timed)
        high, low, flag, ridge = call(
            tile_kernel,
            "tile",
            (half, half, col, col),
            pair, near, every, flag, ridge, timed,
            scalars=1,
            unread=1,
        )

        high, pieces[last] = lax.optimization_barrier((high, pieces[last]))
        first = rows * 1 // 2
        image, one, two = call(
            image_kernel,
            "image",
            (block, shape(first, width), shape(rows - first, width)),
            *over_cfg(pieces, high, low, (0, last), tuple(range(last - 1, 0, -1))), residual,
        )

        ones, twos = far_cfg(over_time(one)), far_cfg(over_time(two, 0, *range(2, tm), 1))
        partial = call(early_rows_kernel, "early_rows", shape(2 * rows, width), *ones, high, low)
        soon = (last + 1) // 2
        partial = call(
            functools.partial(middle_rows_kernel, last + 1),
            "middle_rows",
            shape(2 * rows, width),
            *twos[:soon], partial, high, low,
        )
        own, theirs, sums = call(
            functools.partial(late_rows_kernel, last + 1),
            "late_rows",
            (block, block, shape(cfg * tm, 1, width)),
            *twos[soon:], partial, high, low, ridge, image, near_cfg(image), residual,
        )
        sums = lax.all_to_all(sums, ("cfg", "tm"), 0, 0, tiled=True)
        return call(
            finish_kernel, "finish", (block, block), sums, residual, own, near_cfg(theirs), flag, ridge, image
        )

    return jax.shard_map(
        body,
        mesh=mesh,
        in_specs=(P("cfg", "tm"), P("cfg", None), P(), P("cfg"), P("tm", None), P("cfg", "tm")),
        out_specs=(P("cfg", "tm"), P("cfg", "tm")),
        check_vma=False,
    )
```
